512 devices in a mesh: member: 32 (over x, y), space: 16 (over z, core).
Axes of the slice: x: 4, y: 8, z: 8, core: 2. Of those that a mesh axis runs over, the one named last changes fastest.
Arguments:
- ensemble: float32 [32, 3, 32, 48, 128], P('member', None, 'space')
- obs_cell: int32 [8192], P('space'), may hold values from 0 to 12287
- obs_comp: int32 [8192], P('space'), may hold values from 0 to 2
- obs_value: float32 [8192], replicated, may hold values from -6 to 6
- obs_precision: float32 [8192], replicated, may hold values from 0.3 to 5
- loc_obs: int32 [16384, 128], P(('space', 'member')), may hold values from 0 to 8191
- loc_level: int32 [16384, 128], P(('space', 'member')), may hold values from 1 to 8
Outputs:
- analysis: float32 [32, 3, 32, 48, 128], P('member', None, 'space')
The draws below stay inside these ranges and needn't reach their ends.
Inputs may be any that keep to these rules, and one draw needn't show every extreme that they name: Observation i lies in the slab of index i // 512; obs_cell is x' * 48 * 128 + y * 128 + z with x' counted within that slab.
All inputs are finite; a program needn't handle non-finite values.
Results may differ from the reference program's by a relative error of at most 0.0003.
Values sent between devices are 32-bit elements; how exact they have to be, the bound alone decides.
No kernel may reach another device: no remote copies, remote signals or barrier semaphores. Data moves between devices by JAX's collectives and lax.ppermute only.
A program may use at most 64 MiB of HBM per device.

```python
import math
import jax
import jax.numpy as jnp
from jax import lax

CX = 2
NY = 48
NZ = 128
NOB_DEV = 512
LOC = 128
NS_ITERS = 8
LEVELS = 8
K = 32
NX = 32
NOBS = 8192
NCHUNK = 16384


def box_mean(field, split_axis, reach):
    total = field
    for shift in range(1, reach + 1):
        total = total + jnp.roll(field, shift, split_axis) + jnp.roll(field, -shift, split_axis)
    return total / jnp.sqrt(jnp.float32(2 * reach + 1))


def blended(raw, rough_amp, smooth_amp):
    smooth = box_mean(box_mean(raw, -1, 4), -3, 2)
    return rough_amp * raw + smooth_amp * smooth


def draw_ensemble(key, part):
    first = jax.random.fold_in(key, 11)
    second = jax.random.fold_in(key, 12)
    spots = jnp.arange(NX, dtype=jnp.float32) / max(NX - 1, 1)
    growth = (0.7 * 2.0 ** spots)[:, None, None]
    rough_amp = (1.2 - 0.9 * spots)[:, None, None]
    smooth_amp = (0.3 + 3.0 * spots)[:, None, None]
    height = (jnp.arange(NY, dtype=jnp.float32) + 0.5) / NY * 2.0 - 1.0
    profile = 1.5 * (1.0 - height * height)
    base = jax.random.normal(first, (3, NX, NY, NZ), jnp.float32)
    noise = jax.random.normal(second, (K, 3, NX, NY, NZ), jnp.float32)
    streamwise = (jnp.arange(3) == 0).astype(jnp.float32)[:, None, None, None]
    base = growth * blended(base, rough_amp, smooth_amp) + streamwise * profile[None, None, :, None]
    noise = growth * blended(noise, rough_amp, smooth_amp)
    member_states = base[None] + 0.5 * noise
    return member_states.astype(jnp.float32)


def touch_ends(drawn, own_key, smallest, high):
    longest = drawn.shape.index(max(drawn.shape))
    spots = []
    for shift in (0, 1):
        where = [jax.random.randint(jax.random.fold_in(own_key, axis), (), 0, length) for axis, length in enumerate(drawn.shape)]
        where[longest] = (where[longest] + shift) % drawn.shape[longest]
        spots.append(tuple(where))
    return drawn.at[spots[0]].set(smallest).at[spots[1]].set(high)


def scatter_about(rng, extent, width, most, kind=jnp.bfloat16):
    drawn = width * jax.random.normal(rng, extent, jnp.float32)
    return jnp.clip(drawn, min=-most, max=most).astype(kind)


def setup_inputs(seed: int = 0) -> dict:
    arg_keys = jax.random.split(jax.random.key(seed), 8)
    ensemble = draw_ensemble(jax.random.fold_in(arg_keys[7], 71), 0)
    obs_cell = touch_ends(jax.random.randint(arg_keys[1], (NOBS,), 0, CX * NY * NZ), jax.random.fold_in(arg_keys[1], 1), 0, (CX * NY * NZ) - 1).astype(jnp.int32)
    obs_comp = touch_ends(jax.random.randint(arg_keys[2], (NOBS,), 0, 3), jax.random.fold_in(arg_keys[2], 1), 0, 2).astype(jnp.int32)
    obs_value = scatter_about(arg_keys[3], (NOBS,), 1.0, 6.0, jnp.float32)
    obs_precision = jnp.clip(jnp.exp(jax.random.uniform(arg_keys[4], (NOBS,), jnp.float32, math.log(0.3), math.log(5.0))), 0.3, 5.0)
    loc_obs = touch_ends(jax.random.randint(arg_keys[5], (NCHUNK, LOC), 0, NOBS), jax.random.fold_in(arg_keys[5], 1), 0, NOBS - 1).astype(jnp.int32)
    loc_level = touch_ends(jax.random.randint(arg_keys[6], (NCHUNK, LOC), 1, LEVELS + 1), jax.random.fold_in(arg_keys[6], 1), 1, LEVELS).astype(jnp.int32)
    return {"ensemble": ensemble, "obs_cell": obs_cell, "obs_comp": obs_comp, "obs_value": obs_value, "obs_precision": obs_precision, "loc_obs": loc_obs, "loc_level": loc_level}


PAIRS = ((0, 0), (1, 1), (2, 2), (0, 1), (0, 2), (1, 2))
HIGH = lax.Precision.HIGHEST

def pair_index(first, second):
    for place, pair in enumerate(PAIRS):
        if pair == (first, second) or pair == (second, first):
            return place
    return 0

def pair_weights():
    return jnp.array([1.0, 1.0, 1.0, 2.0, 2.0, 2.0], jnp.float32)[:, None, None, None]

def along_x(field):
    return 0.5 * (field[:, 2:] - field[:, :-2])

def along_y(field):
    rim_extended = jnp.pad(field, ((0, 0), (0, 0), (1, 1), (0, 0)))
    return 0.5 * (rim_extended[:, :, 2:] - rim_extended[:, :, :-2])

def along_z(field):
    return 0.5 * (jnp.roll(field, -1, 3) - jnp.roll(field, 1, 3))

def inner(field):
    return field[:, 1:-1]

def test_filter(field):
    smooth = 0.25 * (field[:, :-2] + 2.0 * field[:, 1:-1] + field[:, 2:])
    return 0.25 * (jnp.roll(smooth, 1, 3) + 2.0 * smooth + jnp.roll(smooth, -1, 3))

def strain(velocity):
    grads = (along_x(velocity), inner(along_y(velocity)), inner(along_z(velocity)))
    return jnp.stack([0.5 * (grads[b][a] + grads[a][b]) for a, b in PAIRS])

def magnitude(rate):
    return jnp.sqrt(2.0 * lax.optimization_barrier(jnp.sum(pair_weights() * rate * rate, 0)))

def eddy_substep(rim_extended, plane_sum, count):
    centre = inner(rim_extended)
    rate = strain(rim_extended)
    size = magnitude(rate)
    smooth = test_filter(rim_extended)
    rate_hat = strain(smooth)
    size_hat = magnitude(rate_hat)
    middle = inner(smooth)
    products = jnp.stack([centre[a] * centre[b] for a, b in PAIRS])
    leonard = test_filter(products) - jnp.stack([middle[a] * middle[b] for a, b in PAIRS])
    model = 2.0 * (test_filter(size[None] * rate) - 4.0 * size_hat[None] * rate_hat)
    weights = pair_weights()
    numer = lax.optimization_barrier(jnp.sum(weights * leonard * model, axis=(0, 1, 3)))
    denom = lax.optimization_barrier(jnp.sum(weights * model * model, axis=(0, 1, 3)))
    numer, denom = plane_sum(numer, denom)
    coeff = numer / count / (denom / count + 1e-06)
    stress = 2.0 * coeff[None, None, :, None] * size[None] * rate
    tendency = []
    for a in range(3):
        term = along_x(stress[pair_index(a, 0)][None])[0]
        term = term + inner(along_y(stress[pair_index(a, 1)][None]))[0]
        term = term + inner(along_z(stress[pair_index(a, 2)][None]))[0]
        tendency.append(term)
    return rim_extended[:, 2:-2] + 0.25 * jnp.stack(tendency)

def bmm(left, right):
    return jnp.einsum('mkc,knc->mnc', left, right, precision=HIGH)

def analyse(block, index, level, anomaly, innov, precision):
    member_states = block.shape[0]
    groups, cols_z = (block.shape[2], block.shape[4])
    cols = index.T
    local = jnp.take(anomaly, cols, axis=1)
    weight = level.T.astype(jnp.float32) / LEVELS * jnp.take(precision, cols)
    scaled = local * weight[None]
    eye = jnp.eye(member_states, dtype=jnp.float32)[:, :, None]
    matrix = jnp.einsum('mjc,njc->mnc', scaled, local, precision=HIGH) + (member_states - 1) / 1.1 * eye
    scale = jnp.sqrt(lax.optimization_barrier(jnp.sum(matrix * matrix, axis=(0, 1))))
    root = matrix / scale
    inverse = jnp.broadcast_to(eye, matrix.shape)
    for sweep in range(NS_ITERS):
        factor = 0.5 * (3.0 * eye - bmm(inverse, root))
        root = bmm(root, factor)
        inverse = bmm(factor, inverse)
    cover = bmm(inverse, inverse) / scale
    drive = jnp.einsum('mjc,jc->mc', scaled, jnp.take(innov, cols), precision=HIGH)
    offset = jnp.einsum('mnc,nc->mc', cover, drive, precision=HIGH)
    transform = jnp.sqrt(member_states - 1.0) * inverse / jnp.sqrt(scale) + offset[:, None, :]
    transform = transform.reshape(member_states, member_states, groups, cols_z // 4)
    transform = jnp.repeat(transform, 4, axis=3)
    centre = lax.optimization_barrier(jnp.mean(block, axis=0))
    spread = block - centre
    moved = jnp.einsum('mqgyz,mkgz->kqgyz', spread, transform, precision=HIGH)
    return centre + moved

def reference(ensemble, obs_cell, obs_comp, obs_value, obs_precision, loc_obs, loc_level):
    member_states = ensemble.shape[0]

    def step_forward(field):
        rim_extended = jnp.concatenate([field[:, -2:], field, field[:, :2]], axis=1)
        return eddy_substep(rim_extended, lambda a, b: (a, b), NX * NZ)
    prior_state = lax.map(step_forward, ensemble)
    grid_cells = NX * NY * NZ
    slab = (jnp.arange(NOBS, dtype=jnp.int32) // NOB_DEV).astype(jnp.int32)
    slab_position = obs_comp * grid_cells + slab * (CX * NY * NZ) + obs_cell
    observed_values = jnp.take(prior_state.reshape(member_states, 3 * grid_cells), slab_position, axis=1)
    mean = lax.optimization_barrier(jnp.mean(observed_values, axis=0))
    anomaly = observed_values - mean[None]
    innov = obs_value - mean
    row_total = NX * NY // 3
    vertical_blocks = NZ // 4
    member_group = 8 if row_total % 8 == 0 else 1
    reshaped_field = prior_state.reshape(member_states, 3, row_total // member_group, member_group, 3, NZ)
    reshaped_field = jnp.transpose(reshaped_field, (2, 0, 1, 3, 4, 5))
    index = loc_obs.reshape(row_total // member_group, member_group * vertical_blocks, LOC)
    level = loc_level.reshape(row_total // member_group, member_group * vertical_blocks, LOC)

    def one(items):
        return analyse(items[0], items[1], items[2], anomaly, innov, obs_precision)
    result = lax.map(one, (reshaped_field, index, level))
    result = jnp.transpose(result, (1, 2, 0, 3, 4, 5))
    return result.reshape(member_states, 3, NX, NY, NZ)
```

```python
import functools

import jax
import jax.numpy as jnp
from jax import lax
from jax.experimental import pallas as pl
from jax.experimental.pallas import tpu as pltpu
from jax.sharding import PartitionSpec as P

NS_ITERS = 8
LEVELS = 8
K = 32
LOC = 128
CHUNKS = 32
ROWS = 16

PAIRS = ((0, 0), (1, 1), (2, 2), (0, 1), (0, 2), (1, 2))
F32 = jnp.float32
BF16 = jnp.bfloat16
VMEM = pl.BlockSpec(memory_space=pltpu.VMEM)
SMEM = pl.BlockSpec(memory_space=pltpu.SMEM)


def iota(shape, dim):
    return lax.broadcasted_iota(jnp.int32, shape, dim)


def pair_index(first, second):
    return PAIRS.index((min(first, second), max(first, second)))


def split2(value):
    high = value.astype(BF16)
    return high, (value - high.astype(F32)).astype(BF16)


def split3(value):
    high = value.astype(BF16)
    rest = value - high.astype(F32)
    middle = rest.astype(BF16)
    return high, middle, (rest - middle.astype(F32)).astype(BF16)


def dot(left, right):
    return jnp.dot(left, right, preferred_element_type=F32)


def dot_t(left, right):
    return lax.dot_general(left, right, (((0,), (0,)), ((), ())), preferred_element_type=F32)


def along_y(plane):
    count = plane.shape[0]
    row = iota(plane.shape, 0)
    later = jnp.where(row == count - 1, 0.0, pltpu.roll(plane, count - 1, 0))
    earlier = jnp.where(row == 0, 0.0, pltpu.roll(plane, 1, 0))
    return 0.5 * (later - earlier)


def along_z(plane):
    count = plane.shape[1]
    return 0.5 * (pltpu.roll(plane, count - 1, 1) - pltpu.roll(plane, 1, 1))


def filter_z(plane):
    count = plane.shape[1]
    return 0.25 * (pltpu.roll(plane, 1, 1) + 2.0 * plane + pltpu.roll(plane, count - 1, 1))


def filter_xz(planes, p):
    return filter_z(0.25 * (planes[p - 1] + 2.0 * planes[p] + planes[p + 1]))


def strain(fields, p):
    grads = []
    for b in range(3):
        if b == 0:
            grads.append([0.5 * (f[p + 1] - f[p - 1]) for f in fields])
        elif b == 1:
            grads.append([along_y(f[p]) for f in fields])
        else:
            grads.append([along_z(f[p]) for f in fields])
    return [0.5 * (grads[b][a] + grads[a][b]) for a, b in PAIRS]


def weighted(terms):
    return terms[0] + terms[1] + terms[2] + 2.0 * (terms[3] + terms[4] + terms[5])


def magnitude(rate):
    return jnp.sqrt(2.0 * weighted([r * r for r in rate]))


def model_kernel(before, own, after, sums, tau):
    fields = [
        {0: before[a, 0], 1: before[a, 1], 2: own[a, 0], 3: own[a, 1], 4: after[a, 0], 5: after[a, 1]}
        for a in range(3)
    ]
    for p in range(1, 5):
        rate = strain(fields, p)
        size = magnitude(rate)
        for i in range(6):
            tau[i, p - 1] = size * rate[i]
    smooth = [{p: filter_xz(f, p) for p in range(1, 5)} for f in fields]
    numer = 0.0
    denom = 0.0
    for p in (2, 3):
        rate = strain(smooth, p)
        size = magnitude(rate)
        top, bottom = [], []
        for i, (a, b) in enumerate(PAIRS):
            product = {q: fields[a][q] * fields[b][q] for q in (p - 1, p, p + 1)}
            leonard = filter_xz(product, p) - smooth[a][p] * smooth[b][p]
            flux = {q: tau[i, q - 1] for q in (p - 1, p, p + 1)}
            model = 2.0 * (filter_xz(flux, p) - 4.0 * size * rate[i])
            top.append(leonard * model)
            bottom.append(model * model)
        numer = numer + weighted(top)
        denom = denom + weighted(bottom)
    pad = jnp.zeros((32, 128), F32)
    both = jnp.concatenate([numer, denom, pad], axis=0).T
    total = jnp.sum(both, axis=0, keepdims=True)
    sums[...] = jnp.broadcast_to(total[None], sums.shape)


def forecast_kernel(count, sums, own, tau, place, lane, send, state):
    total = sums[0]
    for i in range(1, sums.shape[0]):
        total = total + sums[i]
    denom = pltpu.roll(total, 128 - 48, 1)
    coeff = (total / count) / (denom / count + 1e-6)
    coeff = 2.0 * jnp.broadcast_to(coeff, (128, 128)).T[:48]
    stress = [[coeff * tau[i, p] for p in range(4)] for i in range(6)]
    for a in range(3):
        for x in range(2):
            p = x + 1
            along = stress[pair_index(a, 0)]
            term = 0.5 * (along[p + 1] - along[p - 1])
            term = term + along_y(stress[pair_index(a, 1)][p])
            term = term + along_z(stress[pair_index(a, 2)][p])
            start = a * 96 + x * 48
            state[start : start + 48, :] = own[a, x] + 0.25 * term
    values = state[...]
    chosen = (iota((288, 512), 0) == place[...]).astype(F32).astype(BF16)
    first, second, third = split3(values)
    picked = (dot_t(third, chosen) + dot_t(second, chosen)) + dot_t(first, chosen)
    picked = jnp.where(iota((128, 512), 0) == lane[...], picked, 0.0)
    picked = jnp.sum(picked, axis=0, keepdims=True)
    for m in range(K):
        for a in range(3):
            send[m, 3 * a : 3 * a + 3, :] = state[a * 96 + 3 * m : a * 96 + 3 * m + 3, :]
    for q in range(4):
        piece = picked[:, q * 128 : (q + 1) * 128]
        send[:, 9 + q, :] = jnp.broadcast_to(piece, (K, 128))
    send[:, 13:16, :] = jnp.zeros((K, 3, 128), F32)


def table_kernel(received, value, precision, table):
    member = iota((K, 128), 0)
    parts = []
    for q in range(4):
        seen = received[pl.ds(9 + q, K, stride=ROWS), :]
        mean = jnp.sum(seen, axis=0, keepdims=True) * (1.0 / K)
        innov = value[q : q + 1, :] - mean
        root = jnp.sqrt(precision[q : q + 1, :])
        parts.append(jnp.where(member == K - 1, innov, seen - mean) * root)
    block = jnp.concatenate(parts, axis=0).T
    for i in range(table.shape[0]):
        table[i] = block


def block_diagonal(value, mask):
    return jnp.concatenate([value] * 8, axis=0) * mask


def times_blocks(left, right, mask):
    r1, r2 = split2(right)
    l1, l2 = split2(left)
    rows = left.shape[0]
    wide = dot(jnp.concatenate([l1, l2], axis=0), block_diagonal(r1, mask))
    return wide[:rows] + wide[rows:] + dot(l1, block_diagonal(r2, mask))


def exact_times(left, constant):
    rows = left.shape[0]
    wide = dot(jnp.concatenate(split3(left), axis=0), constant)
    return (wide[2 * rows :] + wide[rows : 2 * rows]) + wide[:rows]


def analysis_kernel(places, code, near, far, received, out, table, picked):
    table[0:1024, :] = near[...]
    table[1024:2048, :] = far[...]

    def fetch(c, carry):
        base = pl.multiple_of(c * LOC, LOC)
        target = picked.at[pl.ds(base, LOC)]
        for j in range(LOC):
            target[pl.ds(j, 1), :] = table[pl.ds(places[base + j], 1), :]
        return carry

    lax.fori_loop(0, CHUNKS, fetch, 0)

    columns = jnp.concatenate([code[...], jnp.zeros((96, 128), jnp.int32)], axis=0).T
    quarter = iota((LOC, 128), 1) // 32
    small_quarter = iota((K, 128), 1) // 32
    grams = []
    for c in range(CHUNKS):
        rows = picked[c * LOC : (c + 1) * LOC, :]
        mark = jnp.broadcast_to(columns[:, c : c + 1], (LOC, 128))
        level = (mark & 15).astype(F32) * (1.0 / LEVELS)
        weight = jnp.where((mark >> 4) == quarter, level, 0.0)
        g1, g2 = split2(rows)
        a1, a2 = split2(weight * rows)
        wide = dot_t(a1, jnp.concatenate([g1, g2], axis=1))
        full = wide[:, :128] + wide[:, 128:] + dot_t(a2, g1)
        fold = full[0:32]
        for q in range(1, 4):
            fold = jnp.where(small_quarter == q, full[32 * q : 32 * q + 32], fold)
        fold = fold + pltpu.roll(fold, 64, 1)
        fold = fold + pltpu.roll(fold, 32, 1)
        if c % 4 == 0:
            held = fold
        else:
            held = jnp.where(small_quarter == c % 4, fold, held)
        if c % 4 == 3:
            grams.append(held)
    grams = [jnp.concatenate(grams[2 * g : 2 * g + 2], axis=1) for g in range(4)]

    tall = iota((256, 256), 0)
    wide_lane = iota((256, 256), 1)
    same = (tall // 32) == (wide_lane // 32)
    mask = jnp.where(same, 1.0, 0.0).astype(BF16)
    last = (wide_lane % 32) == 31
    not_last_row = (tall % 32) != 31
    rebuild = jnp.where(last, jnp.where(same & not_last_row, -1.0, 0.0), jnp.where(tall == wide_lane, 1.0, 0.0))
    rebuild = rebuild.astype(BF16)
    member = iota((K, 256), 0)
    eye = jnp.where(member == iota((K, 256), 1) % 32, 1.0, 0.0)

    count = len(grams)
    drive, scale, y, z = [], [], [], []
    for g in range(count):
        gram = grams[g]
        body = jnp.where(member == K - 1, 0.0, gram)
        body = jnp.where(member == K - 1, -jnp.sum(body, axis=0, keepdims=True), body)
        push = jnp.broadcast_to(gram[K - 1 : K, :], (8, 256))
        whole = exact_times(jnp.concatenate([body, push], axis=0), rebuild)
        matrix = whole[:K] + ((K - 1) / 1.1) * eye
        drive.append(whole[K:])
        square = jnp.broadcast_to(jnp.sum(matrix * matrix, axis=0, keepdims=True), (8, 256))
        norm = jnp.sqrt(exact_times(square, mask))
        scale.append(norm)
        y.append(matrix / norm[0:1])
    for sweep in range(NS_ITERS):
        for g in range(count):
            if sweep == 0:
                factor = 1.5 * eye - 0.5 * y[g]
                z[g:] = [factor]
                y[g] = times_blocks(y[g], factor, mask)
                continue
            factor = 1.5 * eye - 0.5 * times_blocks(z[g], y[g], mask)
            if sweep == NS_ITERS - 1:
                z[g] = times_blocks(z[g], factor, mask)
            else:
                both = times_blocks(jnp.concatenate([y[g], z[g]], axis=0), factor, mask)
                y[g], z[g] = both[:K], both[K:]
    total = None
    cells = [received[pl.ds(r, K, stride=ROWS), :] for r in range(9)]
    centres = [jnp.sum(v, axis=0, keepdims=True) * (1.0 / K) for v in cells]
    spreads = [v - m for v, m in zip(cells, centres)]
    spreads = jnp.concatenate(spreads, axis=1)
    h1, h2 = split2(spreads)
    owner = iota((256, 9 * 128), 0) // 32
    chunk = (iota((256, 9 * 128), 1) % 128) // 4
    for g in range(count):
        pull = times_blocks(times_blocks(drive[g], z[g], mask), z[g], mask) / scale[g]
        root = z[g] * (jnp.sqrt(float(K - 1)) / jnp.sqrt(scale[g][0:1]))
        left1, left2 = split2(jnp.concatenate([root, pull], axis=0))
        here = jnp.where(chunk == owner + 8 * g, 1.0, 0.0).astype(BF16)
        right1 = block_diagonal(h1, here)
        right2 = block_diagonal(h2, here)
        rows = left1.shape[0]
        part = dot(jnp.concatenate([left1, left2], axis=0), right1)
        part = part[:rows] + part[rows:] + dot(left1, right2)
        total = part if total is None else total + part
    moved = total[:K] + total[K : K + 1]
    for r in range(9):
        out[pl.ds(r, K, stride=ROWS), :] = moved[:, r * 128 : (r + 1) * 128] + centres[r]
    for r in range(9, ROWS):
        out[pl.ds(r, K, stride=ROWS), :] = jnp.zeros((K, 128), F32)


def call(kernel, shapes, ins, scratch=(), limit=None):
    return pl.pallas_call(
        kernel,
        out_shape=[jax.ShapeDtypeStruct(s, F32) for s in shapes],
        in_specs=ins,
        out_specs=[VMEM] * len(shapes),
        scratch_shapes=list(scratch),
        compiler_params=pltpu.CompilerParams(vmem_limit_bytes=limit),
    )


def shards(ensemble, obs_cell, obs_comp, obs_value, obs_precision, loc_obs, loc_level):
    field = ensemble[0]
    _, depth, height, extent = field.shape
    parts = lax.axis_size("space")
    here = lax.axis_index("space")
    up = [(i, (i + 1) % parts) for i in range(parts)]
    down = [(j, i) for i, j in up]

    slab = loc_obs // 512
    within = loc_obs % 512
    places = (slab // 2) * 128 + ((slab + here) % 2) * 1024 + within % 128
    places = places.reshape(CHUNKS * LOC)
    code = (within // 128) * 16 + loc_level
    place = (obs_comp * (depth * height) + obs_cell // extent).reshape(1, 512)
    lane = (obs_cell % extent).reshape(1, 512)
    value = lax.dynamic_index_in_dim(obs_value.reshape(parts, 4, 128), here, 0, keepdims=False)
    precision = lax.dynamic_index_in_dim(obs_precision.reshape(parts, 4, 128), here, 0, keepdims=False)

    before = lax.ppermute(field, "space", up)
    after = lax.ppermute(field, "space", down)
    sums, tau = call(model_kernel, [(parts, 1, 128), (6, 4, height, extent)], [VMEM] * 3)(before, field, after)
    sums = lax.all_to_all(sums, "space", 0, 0, tiled=True)
    count = depth * parts * extent
    (send,) = call(
        functools.partial(forecast_kernel, count),
        [(K, ROWS, 128)],
        [VMEM] * 5,
        [pltpu.VMEM((3 * depth * height, extent), F32)],
    )(sums, field, tau, place, lane)
    received = lax.all_to_all(send, "member", 0, 0, tiled=True).reshape(K * ROWS, 128)
    (table,) = call(table_kernel, [(parts // 2, 128, 128)], [VMEM] * 3)(received, value, precision)
    same_core = [[2 * i + c for i in range(parts // 2)] for c in range(2)]
    near = lax.all_to_all(table, "space", 0, 0, axis_index_groups=same_core, tiled=True)
    near = near.reshape(parts * 64, 128)
    far = lax.ppermute(near, "space", [(i, i ^ 1) for i in range(parts)])
    (result,) = call(
        analysis_kernel,
        [(K * ROWS, 128)],
        [SMEM] + [VMEM] * 4,
        [pltpu.VMEM((2048, 128), F32), pltpu.VMEM((CHUNKS * LOC, 128), F32)],
        limit=40 * 2**20,
    )(places, code, near, far, received)
    returned = lax.all_to_all(result.reshape(K, ROWS, 128), "member", 0, 0, tiled=True)
    returned = returned[:, :9].reshape(K, 3, 3, 128)
    returned = jnp.transpose(returned, (1, 0, 2, 3))
    return returned.reshape(1, 3, depth, height, extent)


def solution(mesh):
    in_specs = (
        P("member", None, "space", None, None),
        P("space"),
        P("space"),
        P(),
        P(),
        P(("space", "member"), None),
        P(("space", "member"), None),
    )
    out_specs = P("member", None, "space", None, None)
    return jax.shard_map(shards, mesh=mesh, in_specs=in_specs, out_specs=out_specs, check_vma=False)
```

```python
import functools

import jax
import jax.numpy as jnp
from jax import lax
from jax.experimental import pallas as pl
from jax.experimental.pallas import tpu as pltpu
from jax.sharding import PartitionSpec as P

NS_ITERS = 8
LEVELS = 8
K = 32
LOC = 128
CHUNKS = 32
ROWS = 41
LINES = 21
BACK = 9

PAIRS = ((0, 0), (1, 1), (2, 2), (0, 1), (0, 2), (1, 2))
F32 = jnp.float32
BF16 = jnp.bfloat16
VMEM = pl.BlockSpec(memory_space=pltpu.VMEM)
SMEM = pl.BlockSpec(memory_space=pltpu.SMEM)


def iota(shape, dim):
    return lax.broadcasted_iota(jnp.int32, shape, dim)


def pair_index(first, second):
    return PAIRS.index((min(first, second), max(first, second)))


def split2(value):
    high = value.astype(BF16)
    return high, (value - high.astype(F32)).astype(BF16)


def split3(value):
    high = value.astype(BF16)
    rest = value - high.astype(F32)
    middle = rest.astype(BF16)
    return high, middle, (rest - middle.astype(F32)).astype(BF16)


def dot(left, right):
    return jnp.dot(left, right, preferred_element_type=F32)


def dot_t(left, right):
    return lax.dot_general(left, right, (((0,), (0,)), ((), ())), preferred_element_type=F32)


def along_y(plane):
    count = plane.shape[0]
    row = iota(plane.shape, 0)
    later = jnp.where(row == count - 1, 0.0, pltpu.roll(plane, count - 1, 0))
    earlier = jnp.where(row == 0, 0.0, pltpu.roll(plane, 1, 0))
    return 0.5 * (later - earlier)


def along_z(plane):
    count = plane.shape[1]
    return 0.5 * (pltpu.roll(plane, count - 1, 1) - pltpu.roll(plane, 1, 1))


def filter_z(plane):
    count = plane.shape[1]
    return 0.25 * (pltpu.roll(plane, 1, 1) + 2.0 * plane + pltpu.roll(plane, count - 1, 1))


def filter_xz(planes, p):
    return filter_z(0.25 * (planes[p - 1] + 2.0 * planes[p] + planes[p + 1]))


def strain(fields, p):
    grads = []
    for b in range(3):
        if b == 0:
            grads.append([0.5 * (f[p + 1] - f[p - 1]) for f in fields])
        elif b == 1:
            grads.append([along_y(f[p]) for f in fields])
        else:
            grads.append([along_z(f[p]) for f in fields])
    return [0.5 * (grads[b][a] + grads[a][b]) for a, b in PAIRS]


def weighted(terms):
    return terms[0] + terms[1] + terms[2] + 2.0 * (terms[3] + terms[4] + terms[5])


def magnitude(rate):
    return jnp.sqrt(2.0 * weighted([r * r for r in rate]))


def shifted_y(plane, step):
    count = plane.shape[0]
    row = iota(plane.shape, 0)
    if step > 0:
        return jnp.where(row == count - 1, 0.0, pltpu.roll(plane, count - 1, 0))
    return jnp.where(row == 0, 0.0, pltpu.roll(plane, 1, 0))


def model_kernel(before, own, after, place, lane, level, message, terms):
    fields = [
        {0: before[a, 0], 1: before[a, 1], 2: own[a, 0], 3: own[a, 1], 4: after[a, 0], 5: after[a, 1]}
        for a in range(3)
    ]
    tau = [{} for _ in PAIRS]
    for p in range(1, 5):
        rate = strain(fields, p)
        size = magnitude(rate)
        for i in range(6):
            tau[i][p] = size * rate[i]
    for a in range(3):
        for x in range(2):
            p = x + 2
            start = a * 96 + x * 48
            along = tau[pair_index(a, 0)]
            flat = 0.5 * (along[p + 1] - along[p - 1]) + along_z(tau[pair_index(a, 2)][p])
            upright = 0.25 * tau[pair_index(a, 1)][p]
            terms[0, start : start + 48, :] = 0.5 * flat
            terms[1, start : start + 48, :] = shifted_y(upright, 1)
            terms[2, start : start + 48, :] = -shifted_y(upright, -1)
    chosen = (iota((288, 512), 0) == place[...]).astype(F32).astype(BF16)
    spot = iota((128, 512), 0) == lane[...]
    lines = []
    for f in range(4):
        if f == 0:
            pieces = split3(own[...].reshape(288, 128))
        else:
            pieces = split2(terms[f - 1])
        picked = dot_t(pieces[-1], chosen)
        for piece in pieces[-2::-1]:
            picked = picked + dot_t(piece, chosen)
        lines.append(jnp.sum(jnp.where(spot, picked, 0.0), axis=0, keepdims=True))
    lines.append(level[...])
    smooth = [{p: filter_xz(f, p) for p in range(1, 5)} for f in fields]
    numer = 0.0
    denom = 0.0
    for p in (2, 3):
        rate = strain(smooth, p)
        size = magnitude(rate)
        top, bottom = [], []
        for i, (a, b) in enumerate(PAIRS):
            product = {q: fields[a][q] * fields[b][q] for q in (p - 1, p, p + 1)}
            leonard = filter_xz(product, p) - smooth[a][p] * smooth[b][p]
            model = 2.0 * (filter_xz(tau[i], p) - 4.0 * size * rate[i])
            top.append(leonard * model)
            bottom.append(model * model)
        numer = numer + weighted(top)
        denom = denom + weighted(bottom)
    pad = jnp.zeros((32, 128), F32)
    both = jnp.concatenate([numer, denom, pad], axis=0).T
    total = jnp.sum(both, axis=0, keepdims=True)
    rows = [line[:, q * 128 : (q + 1) * 128] for line in lines for q in range(4)]
    block = jnp.concatenate(rows + [total], axis=0)
    for i in range(message.shape[0] // LINES):
        message[i * LINES : (i + 1) * LINES, :] = block


def forecast_kernel(count, core, message, own, terms, send, state):
    parts = message.shape[0] // LINES
    total = jnp.sum(message[pl.ds(LINES - 1, parts, stride=LINES), :], axis=0, keepdims=True)
    denom = pltpu.roll(total, 128 - 48, 1)
    coeff = (total / count) / (denom / count + 1e-6)
    coeff = jnp.where(iota((1, 128), 1) < 48, coeff, 0.0)
    column = jnp.broadcast_to(coeff, (128, 128)).T[:48]
    upper = shifted_y(column, 1)
    lower = shifted_y(column, -1)
    for a in range(3):
        for x in range(2):
            start = a * 96 + x * 48
            end = start + 48
            change = column * terms[0, start:end, :]
            change = change + (upper * terms[1, start:end, :] + lower * terms[2, start:end, :])
            state[start:end, :] = own[a, x] + change
    odd = core[0] == 1
    flow, height = [], []

    def lines(f):
        pieces = []
        for i in range(parts // 2):
            even_at = 2 * i * LINES + 4 * f
            odd_at = even_at + LINES
            pieces.append(jnp.where(odd, message[odd_at : odd_at + 4, :], message[even_at : even_at + 4, :]))
        return jnp.concatenate(pieces, axis=0)

    height = lines(4).astype(jnp.int32)
    table = jnp.broadcast_to(coeff, height.shape)

    def look(where):
        where = jnp.clip(where, 0, 127)
        return jnp.take_along_axis(table, where, axis=1)

    seen = lines(0) + look(height) * lines(1)
    seen = seen + (look(height + 1) * lines(2) + look(height - 1) * lines(3))
    for m in range(K):
        base = m * ROWS
        for a in range(3):
            send[base + 3 * a : base + 3 * a + 3, :] = state[a * 96 + 3 * m : a * 96 + 3 * m + 3, :]
        send[base + 9 : base + ROWS, :] = seen


def table_kernel(received, value, precision, table):
    member = iota((K, 128), 0)
    for i in range(8):
        parts = []
        for q in range(4):
            r = 4 * i + q
            seen = received[pl.ds(9 + r, K, stride=ROWS), :]
            mean = jnp.sum(seen, axis=0, keepdims=True) * (1.0 / K)
            innov = value[r : r + 1, :] - mean
            root = jnp.sqrt(precision[r : r + 1, :])
            parts.append(jnp.where(member == K - 1, innov, seen - mean) * root)
        table[i * 128 : (i + 1) * 128, :] = jnp.concatenate(parts, axis=0).T


def block_diagonal(value, mask):
    return jnp.concatenate([value] * 8, axis=0) * mask


def times_blocks(left, right, mask):
    r1, r2 = split2(right)
    l1, l2 = split2(left)
    rows = left.shape[0]
    wide = dot(jnp.concatenate([l1, l2], axis=0), block_diagonal(r1, mask))
    return wide[:rows] + wide[rows:] + dot(l1, block_diagonal(r2, mask))


def exact_times(left, constant):
    rows = left.shape[0]
    wide = dot(jnp.concatenate(split3(left), axis=0), constant)
    return (wide[2 * rows :] + wide[rows : 2 * rows]) + wide[:rows]


def analysis_kernel(places, code, near, far, received, out, table, picked):
    table[0:1024, :] = near[...]
    table[1024:2048, :] = far[...]

    def fetch(c, carry):
        base = pl.multiple_of(c * LOC, LOC)
        target = picked.at[pl.ds(base, LOC)]
        for j in range(LOC):
            target[pl.ds(j, 1), :] = table[pl.ds(places[base + j], 1), :]
        return carry

    lax.fori_loop(0, CHUNKS, fetch, 0)

    columns = jnp.concatenate([code[...], jnp.zeros((96, 128), jnp.int32)], axis=0).T
    quarter = iota((LOC, 128), 1) // 32
    small_quarter = iota((K, 128), 1) // 32
    grams = []
    for c in range(CHUNKS):
        rows = picked[c * LOC : (c + 1) * LOC, :]
        mark = jnp.broadcast_to(columns[:, c : c + 1], (LOC, 128))
        level = (mark & 15).astype(F32) * (1.0 / LEVELS)
        weight = jnp.where((mark >> 4) == quarter, level, 0.0)
        g1, g2 = split2(rows)
        a1, a2 = split2(weight * rows)
        wide = dot_t(a1, jnp.concatenate([g1, g2], axis=1))
        full = wide[:, :128] + wide[:, 128:] + dot_t(a2, g1)
        fold = full[0:32]
        for q in range(1, 4):
            fold = jnp.where(small_quarter == q, full[32 * q : 32 * q + 32], fold)
        fold = fold + pltpu.roll(fold, 64, 1)
        fold = fold + pltpu.roll(fold, 32, 1)
        if c % 4 == 0:
            held = fold
        else:
            held = jnp.where(small_quarter == c % 4, fold, held)
        if c % 4 == 3:
            grams.append(held)
    grams = [jnp.concatenate(grams[2 * g : 2 * g + 2], axis=1) for g in range(4)]

    tall = iota((256, 256), 0)
    wide_lane = iota((256, 256), 1)
    same = (tall // 32) == (wide_lane // 32)
    mask = jnp.where(same, 1.0, 0.0).astype(BF16)
    last = (wide_lane % 32) == 31
    not_last_row = (tall % 32) != 31
    rebuild = jnp.where(last, jnp.where(same & not_last_row, -1.0, 0.0), jnp.where(tall == wide_lane, 1.0, 0.0))
    rebuild = rebuild.astype(BF16)
    member = iota((K, 256), 0)
    eye = jnp.where(member == iota((K, 256), 1) % 32, 1.0, 0.0)

    count = len(grams)
    drive, scale, y, z = [], [], [], []
    for g in range(count):
        gram = grams[g]
        body = jnp.where(member == K - 1, 0.0, gram)
        body = jnp.where(member == K - 1, -jnp.sum(body, axis=0, keepdims=True), body)
        push = jnp.broadcast_to(gram[K - 1 : K, :], (8, 256))
        whole = exact_times(jnp.concatenate([body, push], axis=0), rebuild)
        matrix = whole[:K] + ((K - 1) / 1.1) * eye
        drive.append(whole[K:])
        square = jnp.broadcast_to(jnp.sum(matrix * matrix, axis=0, keepdims=True), (8, 256))
        norm = jnp.sqrt(exact_times(square, mask))
        scale.append(norm)
        y.append(matrix / norm[0:1])
    for sweep in range(NS_ITERS):
        for g in range(count):
            if sweep == 0:
                factor = 1.5 * eye - 0.5 * y[g]
                z[g:] = [factor]
                y[g] = times_blocks(y[g], factor, mask)
                continue
            factor = 1.5 * eye - 0.5 * times_blocks(z[g], y[g], mask)
            if sweep == NS_ITERS - 1:
                z[g] = times_blocks(z[g], factor, mask)
            else:
                both = times_blocks(jnp.concatenate([y[g], z[g]], axis=0), factor, mask)
                y[g], z[g] = both[:K], both[K:]
    total = None
    cells = [received[pl.ds(r, K, stride=ROWS), :] for r in range(9)]
    centres = [jnp.sum(v, axis=0, keepdims=True) * (1.0 / K) for v in cells]
    spreads = [v - m for v, m in zip(cells, centres)]
    spreads = jnp.concatenate(spreads, axis=1)
    h1, h2 = split2(spreads)
    owner = iota((256, 9 * 128), 0) // 32
    chunk = (iota((256, 9 * 128), 1) % 128) // 4
    for g in range(count):
        pull = times_blocks(times_blocks(drive[g], z[g], mask), z[g], mask) / scale[g]
        root = z[g] * (jnp.sqrt(float(K - 1)) / jnp.sqrt(scale[g][0:1]))
        left1, left2 = split2(jnp.concatenate([root, pull], axis=0))
        here = jnp.where(chunk == owner + 8 * g, 1.0, 0.0).astype(BF16)
        right1 = block_diagonal(h1, here)
        right2 = block_diagonal(h2, here)
        rows = left1.shape[0]
        part = dot(jnp.concatenate([left1, left2], axis=0), right1)
        part = part[:rows] + part[rows:] + dot(left1, right2)
        total = part if total is None else total + part
    moved = total[:K] + total[K : K + 1]
    for r in range(9):
        out[pl.ds(r, K, stride=BACK), :] = moved[:, r * 128 : (r + 1) * 128] + centres[r]


def order_kernel(returned, out):
    for m in range(K):
        x, y = m // 16, 3 * (m % 16)
        for a in range(3):
            out[a, x, y : y + 3, :] = returned[m * BACK + 3 * a : m * BACK + 3 * a + 3, :]


def call(kernel, shapes, ins, scratch=(), limit=24 * 2**20):
    return pl.pallas_call(
        kernel,
        out_shape=[jax.ShapeDtypeStruct(s, F32) for s in shapes],
        in_specs=ins,
        out_specs=[VMEM] * len(shapes),
        scratch_shapes=list(scratch),
        compiler_params=pltpu.CompilerParams(vmem_limit_bytes=limit),
    )


def exchange(rows, axis, count):
    width = rows.size // count
    sent = lax.all_to_all(rows.reshape(count, 1, width), axis, 0, 0, tiled=True)
    return sent.reshape(rows.shape)


def shards(ensemble, obs_cell, obs_comp, obs_value, obs_precision, loc_obs, loc_level):
    field = ensemble[0]
    _, depth, height, extent = field.shape
    parts = lax.axis_size("space")
    here = lax.axis_index("space")
    up = [(i, (i + 1) % parts) for i in range(parts)]
    down = [(j, i) for i, j in up]

    slab = loc_obs // 512
    within = loc_obs % 512
    places = (slab // 2) * 128 + ((slab + here) % 2) * 1024 + within % 128
    places = places.reshape(CHUNKS * LOC)
    code = (within // 128) * 16 + loc_level
    place = (obs_comp * (depth * height) + obs_cell // extent).reshape(1, 512)
    lane = (obs_cell % extent).reshape(1, 512)
    level = ((obs_cell // extent) % height).astype(F32).reshape(1, 512)
    core = here & 1
    value = lax.dynamic_index_in_dim(obs_value.reshape(parts // 2, 2, 4, 128), core, 1, keepdims=False)
    value = value.reshape(K, 128)
    precision = lax.dynamic_index_in_dim(obs_precision.reshape(parts // 2, 2, 4, 128), core, 1, keepdims=False)
    precision = precision.reshape(K, 128)

    before = lax.ppermute(field, "space", up)
    after = lax.ppermute(field, "space", down)
    message, terms = call(
        model_kernel, [(parts * LINES, 128), (3, 3 * depth * height, extent)], [VMEM] * 6
    )(before, field, after, place, lane, level)
    message = exchange(message, "space", parts)
    (send,) = call(
        functools.partial(forecast_kernel, depth * parts * extent),
        [(K * ROWS, 128)],
        [SMEM] + [VMEM] * 3,
        [pltpu.VMEM((3 * depth * height, extent), F32)],
    )(core.reshape(1), message, field, terms)
    received = exchange(send, "member", K)
    (near,) = call(table_kernel, [(parts * 64, 128)], [VMEM] * 3)(received, value, precision)
    far = lax.ppermute(near, "space", [(i, i ^ 1) for i in range(parts)])
    (result,) = call(
        analysis_kernel,
        [(K * BACK, 128)],
        [SMEM] + [VMEM] * 4,
        [pltpu.VMEM((2048, 128), F32), pltpu.VMEM((CHUNKS * LOC, 128), F32)],
        limit=40 * 2**20,
    )(places, code, near, far, received)
    returned = exchange(result, "member", K)
    (result,) = call(order_kernel, [(3, depth, height, extent)], [VMEM])(returned)
    return result[None]


def solution(mesh):
    in_specs = (
        P("member", None, "space", None, None),
        P("space"),
        P("space"),
        P(),
        P(),
        P(("space", "member"), None),
        P(("space", "member"), None),
    )
    out_specs = P("member", None, "space", None, None)
    return jax.shard_map(shards, mesh=mesh, in_specs=in_specs, out_specs=out_specs, check_vma=False)
```

```python
import functools

import jax
import jax.numpy as jnp
from jax import lax
from jax.experimental import pallas as pl
from jax.experimental.pallas import tpu as pltpu
from jax.sharding import PartitionSpec as P

NS_ITERS = 8
LEVELS = 8
K = 32
LOC = 128
CHUNKS = 32
ROWS = 41
LINES = 24
BACK = 9

PAIRS = ((0, 0), (1, 1), (2, 2), (0, 1), (0, 2), (1, 2))
F32 = jnp.float32
BF16 = jnp.bfloat16
VMEM = pl.BlockSpec(memory_space=pltpu.VMEM)
SMEM = pl.BlockSpec(memory_space=pltpu.SMEM)


def iota(shape, dim):
    return lax.broadcasted_iota(jnp.int32, shape, dim)


def pair_index(first, second):
    return PAIRS.index((min(first, second), max(first, second)))


def split2(value):
    high = value.astype(BF16)
    return high, (value - high.astype(F32)).astype(BF16)


def split3(value):
    high = value.astype(BF16)
    rest = value - high.astype(F32)
    middle = rest.astype(BF16)
    return high, middle, (rest - middle.astype(F32)).astype(BF16)


def dot(left, right):
    return jnp.dot(left, right, preferred_element_type=F32)


def dot_t(left, right):
    return lax.dot_general(left, right, (((0,), (0,)), ((), ())), preferred_element_type=F32)


def along_y(plane):
    count = plane.shape[0]
    row = iota(plane.shape, 0)
    later = jnp.where(row == count - 1, 0.0, pltpu.roll(plane, count - 1, 0))
    earlier = jnp.where(row == 0, 0.0, pltpu.roll(plane, 1, 0))
    return 0.5 * (later - earlier)


def along_z(plane):
    count = plane.shape[1]
    return 0.5 * (pltpu.roll(plane, count - 1, 1) - pltpu.roll(plane, 1, 1))


def filter_z(plane):
    count = plane.shape[1]
    return 0.25 * (pltpu.roll(plane, 1, 1) + 2.0 * plane + pltpu.roll(plane, count - 1, 1))


def filter_xz(planes, p):
    return filter_z(0.25 * (planes[p - 1] + 2.0 * planes[p] + planes[p + 1]))


def strain(fields, p):
    grads = []
    for b in range(3):
        if b == 0:
            grads.append([0.5 * (f[p + 1] - f[p - 1]) for f in fields])
        elif b == 1:
            grads.append([along_y(f[p]) for f in fields])
        else:
            grads.append([along_z(f[p]) for f in fields])
    return [0.5 * (grads[b][a] + grads[a][b]) for a, b in PAIRS]


def weighted(terms):
    return terms[0] + terms[1] + terms[2] + 2.0 * (terms[3] + terms[4] + terms[5])


def magnitude(rate):
    return jnp.sqrt(2.0 * weighted([r * r for r in rate]))


def shifted_y(plane, step):
    count = plane.shape[0]
    row = iota(plane.shape, 0)
    if step > 0:
        return jnp.where(row == count - 1, 0.0, pltpu.roll(plane, count - 1, 0))
    return jnp.where(row == 0, 0.0, pltpu.roll(plane, 1, 0))


def model_kernel(before, own, after, place, lane, level, message, terms):
    fields = [
        {0: before[a, 0], 1: before[a, 1], 2: own[a, 0], 3: own[a, 1], 4: after[a, 0], 5: after[a, 1]}
        for a in range(3)
    ]
    tau = [{} for _ in PAIRS]
    for p in range(1, 5):
        rate = strain(fields, p)
        size = magnitude(rate)
        for i in range(6):
            tau[i][p] = size * rate[i]
    for a in range(3):
        for x in range(2):
            p = x + 2
            start = a * 96 + x * 48
            along = tau[pair_index(a, 0)]
            flat = 0.5 * (along[p + 1] - along[p - 1]) + along_z(tau[pair_index(a, 2)][p])
            upright = 0.25 * tau[pair_index(a, 1)][p]
            terms[0, start : start + 48, :] = 0.5 * flat
            terms[1, start : start + 48, :] = shifted_y(upright, 1)
            terms[2, start : start + 48, :] = -shifted_y(upright, -1)
    chosen = (iota((288, 512), 0) == place[...]).astype(F32).astype(BF16)
    spot = iota((128, 512), 0) == lane[...]
    lines = []
    for f in range(4):
        if f == 0:
            pieces = split3(own[...].reshape(288, 128))
        else:
            pieces = split2(terms[f - 1])
        picked = dot_t(pieces[-1], chosen)
        for piece in pieces[-2::-1]:
            picked = picked + dot_t(piece, chosen)
        lines.append(jnp.sum(jnp.where(spot, picked, 0.0), axis=0, keepdims=True))
    lines.append(level[...])
    smooth = [{p: filter_xz(f, p) for p in range(1, 5)} for f in fields]
    numer = 0.0
    denom = 0.0
    for p in (2, 3):
        rate = strain(smooth, p)
        size = magnitude(rate)
        top, bottom = [], []
        for i, (a, b) in enumerate(PAIRS):
            product = {q: fields[a][q] * fields[b][q] for q in (p - 1, p, p + 1)}
            leonard = filter_xz(product, p) - smooth[a][p] * smooth[b][p]
            model = 2.0 * (filter_xz(tau[i], p) - 4.0 * size * rate[i])
            top.append(leonard * model)
            bottom.append(model * model)
        numer = numer + weighted(top)
        denom = denom + weighted(bottom)
    pad = jnp.zeros((32, 128), F32)
    both = jnp.concatenate([numer, denom, pad], axis=0).T
    total = jnp.sum(both, axis=0, keepdims=True)
    rows = [line[:, q * 128 : (q + 1) * 128] for line in lines for q in range(4)]
    block = jnp.concatenate(rows + [total, jnp.zeros((3, 128), F32)], axis=0)
    for i in range(message.shape[0] // LINES):
        message[i * LINES : (i + 1) * LINES, :] = block


def forecast_kernel(count, core, message, own, terms, send, state):
    parts = message.shape[0] // LINES
    total = jnp.sum(message[pl.ds(20, parts, stride=LINES), :], axis=0, keepdims=True)
    denom = pltpu.roll(total, 128 - 48, 1)
    coeff = (total / count) / (denom / count + 1e-6)
    coeff = jnp.where(iota((1, 128), 1) < 48, coeff, 0.0)
    column = jnp.broadcast_to(coeff, (128, 128)).T[:48]
    upper = shifted_y(column, 1)
    lower = shifted_y(column, -1)
    for a in range(3):
        for x in range(2):
            start = a * 96 + x * 48
            end = start + 48
            change = column * terms[0, start:end, :]
            change = change + (upper * terms[1, start:end, :] + lower * terms[2, start:end, :])
            state[start:end, :] = own[a, x] + change
    odd = core[0] == 1
    flow, height = [], []

    def lines(f):
        pieces = []
        for i in range(parts // 2):
            even_at = 2 * i * LINES + 4 * f
            odd_at = even_at + LINES
            pieces.append(jnp.where(odd, message[odd_at : odd_at + 4, :], message[even_at : even_at + 4, :]))
        return jnp.concatenate(pieces, axis=0)

    height = lines(4).astype(jnp.int32)
    table = jnp.broadcast_to(coeff, height.shape)

    def look(where):
        where = jnp.clip(where, 0, 127)
        return jnp.take_along_axis(table, where, axis=1)

    seen = lines(0) + look(height) * lines(1)
    seen = seen + (look(height + 1) * lines(2) + look(height - 1) * lines(3))
    for m in range(K):
        base = m * ROWS
        for a in range(3):
            send[base + 3 * a : base + 3 * a + 3, :] = state[a * 96 + 3 * m : a * 96 + 3 * m + 3, :]
        send[base + 9 : base + ROWS, :] = seen


def table_kernel(received, value, precision, table):
    member = iota((K, 128), 0)
    for i in range(8):
        parts = []
        for q in range(4):
            r = 4 * i + q
            seen = received[pl.ds(9 + r, K, stride=ROWS), :]
            mean = jnp.sum(seen, axis=0, keepdims=True) * (1.0 / K)
            innov = value[r : r + 1, :] - mean
            root = jnp.sqrt(precision[r : r + 1, :])
            parts.append(jnp.where(member == K - 1, innov, seen - mean) * root)
        table[i * 128 : (i + 1) * 128, :] = jnp.concatenate(parts, axis=0).T


def block_diagonal(value, mask):
    return jnp.concatenate([value] * 8, axis=0) * mask


def times_blocks(left, right, mask):
    r1, r2 = split2(right)
    l1, l2 = split2(left)
    rows = left.shape[0]
    wide = dot(jnp.concatenate([l1, l2], axis=0), block_diagonal(r1, mask))
    return wide[:rows] + wide[rows:] + dot(l1, block_diagonal(r2, mask))


def exact_times(left, constant):
    rows = left.shape[0]
    wide = dot(jnp.concatenate(split3(left), axis=0), constant)
    return (wide[2 * rows :] + wide[rows : 2 * rows]) + wide[:rows]


def copy_kernel(source, target):
    pltpu.sync_copy(source, target)


def weight_kernel(code, weights):
    columns = jnp.concatenate([code[...], jnp.zeros((96, 128), jnp.int32)], axis=0).T
    quarter = iota((LOC, 128), 1) // 32
    for c in range(CHUNKS):
        mark = jnp.broadcast_to(columns[:, c : c + 1], (LOC, 128))
        level = jnp.sqrt((mark & 15).astype(F32) * (1.0 / LEVELS))
        weights[c * LOC : (c + 1) * LOC, :] = jnp.where((mark >> 4) == quarter, level, 0.0)


def spread_kernel(received, tiles, centres):
    cells = [received[pl.ds(r, K, stride=ROWS), :] for r in range(9)]
    means = [jnp.sum(v, axis=0, keepdims=True) * (1.0 / K) for v in cells]
    centres[...] = jnp.concatenate(means, axis=0)
    spreads = [v - m for v, m in zip(cells, means)]
    owner = iota((256, 288), 0) // 32
    chunk = (iota((256, 288), 1) % 32) // 4
    here = jnp.where(chunk == owner, 1.0, 0.0).astype(BF16)
    for g in range(4):
        packed = jnp.concatenate([v[:, 32 * g : 32 * g + 32] for v in spreads], axis=1)
        h1, h2 = split2(packed)
        tiles[g, :, 0:288] = block_diagonal(h1, here)
        tiles[g, :, 288:576] = block_diagonal(h2, here)


def folded(rows, weights):
    lone = rows * weights
    lone = lone + pltpu.roll(lone, 64, 1)
    return lone + pltpu.roll(lone, 32, 1)


def four_gram(pack):
    quarter = iota((LOC, 128), 1) // 32
    high, low = split2(pack)
    blocks = [jnp.where(quarter == i, 1.0, 0.0).astype(BF16) for i in range(4)]
    right1 = jnp.concatenate([high * b for b in blocks], axis=0)
    right2 = jnp.concatenate([low * b for b in blocks], axis=0)
    turned = pack.T
    turned = jnp.concatenate([turned[32 * i : 32 * i + 32] for i in range(4)], axis=1)
    left1, left2 = split2(turned)
    wide = dot(jnp.concatenate([left1, left2], axis=0), right1)
    return (wide[K:] + dot(left1, right2)) + wide[:K]


def analysis_kernel(places, weights, near, far, tiles, centres, out, table, first, second, grams):
    table[0:1024, :] = near[...]
    table[1024:2048, :] = far[...]

    quarter = iota((LOC, 128), 1) // 32

    def fetch(c, target, at):
        base = c * LOC
        for j in range(LOC):
            target[at + j : at + j + 1, :] = table[pl.ds(places[base + j], 1), :]

    def half(four, source, target):
        coming = jnp.minimum(4 * four + 4, CHUNKS - 4)
        pack = None
        for i in range(4):
            fetch(coming + i, target, i * LOC)
            at = pl.multiple_of(four * (4 * LOC) + i * LOC, LOC)
            lone = folded(source[i * LOC : (i + 1) * LOC, :], weights[pl.ds(at, LOC), :])
            pack = lone if i == 0 else jnp.where(quarter == i, lone, pack)
        grams[four] = four_gram(pack)

    for i in range(4):
        fetch(i, first, i * LOC)

    def step(i, carry):
        half(2 * i, first, second)
        half(2 * i + 1, second, first)
        return carry

    lax.fori_loop(0, 4, step, 0)
    packs = [jnp.concatenate([grams[2 * g], grams[2 * g + 1]], axis=1) for g in range(4)]

    tall = iota((256, 256), 0)
    wide_lane = iota((256, 256), 1)
    same = (tall // 32) == (wide_lane // 32)
    mask = jnp.where(same, 1.0, 0.0).astype(BF16)
    last = (wide_lane % 32) == 31
    not_last_row = (tall % 32) != 31
    rebuild = jnp.where(last, jnp.where(same & not_last_row, -1.0, 0.0), jnp.where(tall == wide_lane, 1.0, 0.0))
    rebuild = rebuild.astype(BF16)
    member = iota((K, 256), 0)
    eye = jnp.where(member == iota((K, 256), 1) % 32, 1.0, 0.0)

    count = len(packs)
    drive, scale, y, z = [], [], [], []
    for g in range(count):
        pack = packs[g]
        body = jnp.where(member == K - 1, 0.0, pack)
        body = jnp.where(member == K - 1, -jnp.sum(body, axis=0, keepdims=True), body)
        push = jnp.broadcast_to(pack[K - 1 : K, :], (16, 256))
        whole = exact_times(jnp.concatenate([body, push], axis=0), rebuild)
        matrix = whole[:K] + ((K - 1) / 1.1) * eye
        drive.append(whole[K:])
        square = jnp.broadcast_to(jnp.sum(matrix * matrix, axis=0, keepdims=True), (16, 256))
        norm = jnp.sqrt(exact_times(square, mask))
        scale.append(norm)
        y.append(matrix / norm[0:1])
    for sweep in range(NS_ITERS):
        for g in range(count):
            if sweep == 0:
                factor = 1.5 * eye - 0.5 * y[g]
                both = times_blocks(jnp.concatenate([y[g], drive[g]], axis=0), factor, mask)
                y[g], drive[g] = both[:K], both[K:]
                z.append(factor)
                continue
            factor = 1.5 * eye - 0.5 * times_blocks(z[g], y[g], mask)
            if sweep == NS_ITERS - 1:
                both = times_blocks(jnp.concatenate([z[g], drive[g]], axis=0), factor, mask)
                z[g], drive[g] = both[:K], both[K:]
            else:
                both = times_blocks(jnp.concatenate([y[g], z[g], drive[g]], axis=0), factor, mask)
                y[g], z[g], drive[g] = both[:K], both[K : 2 * K], both[2 * K :]
    moved = []
    for g in range(count):
        pull = times_blocks(drive[g], z[g], mask) / scale[g]
        root = z[g] * (jnp.sqrt(float(K - 1)) / jnp.sqrt(scale[g][0:1]))
        left1, left2 = split2(jnp.concatenate([root, pull], axis=0))
        rows = left1.shape[0]
        part = dot(jnp.concatenate([left1, left2], axis=0), tiles[g])
        part = part[:rows, :288] + part[rows:, :288] + part[:rows, 288:]
        moved.append(part[:K] + part[K : K + 1])
    for r in range(9):
        row = jnp.concatenate([part[:, 32 * r : 32 * r + 32] for part in moved], axis=1)
        out[pl.ds(r, K, stride=BACK), :] = row + centres[r : r + 1, :]


SCRATCH = [
    pltpu.VMEM((2048, 128), F32),
    pltpu.VMEM((4 * LOC, 128), F32),
    pltpu.VMEM((4 * LOC, 128), F32),
    pltpu.VMEM((CHUNKS // 4, K, 128), F32),
]


def order_kernel(returned, out):
    for m in range(K):
        x, y = m // 16, 3 * (m % 16)
        for a in range(3):
            out[a, x, y : y + 3, :] = returned[m * BACK + 3 * a : m * BACK + 3 * a + 3, :]


def call(kernel, shapes, ins, scratch=(), limit=24 * 2**20, kinds=None):
    return pl.pallas_call(
        kernel,
        out_shape=[jax.ShapeDtypeStruct(s, t) for s, t in zip(shapes, kinds or [F32] * len(shapes))],
        in_specs=ins,
        out_specs=[VMEM] * len(shapes),
        scratch_shapes=list(scratch),
        compiler_params=pltpu.CompilerParams(vmem_limit_bytes=limit),
    )


def exchange(rows, axis, count):
    width = rows.size // count
    sent = lax.all_to_all(rows.reshape(count, 1, width), axis, 0, 0, tiled=True)
    return sent.reshape(rows.shape)


def shards(ensemble, obs_cell, obs_comp, obs_value, obs_precision, loc_obs, loc_level):
    field = ensemble[0]
    _, depth, height, extent = field.shape
    parts = lax.axis_size("space")
    here = lax.axis_index("space")
    up = [(i, (i + 1) % parts) for i in range(parts)]
    down = [(j, i) for i, j in up]

    slab = loc_obs // 512
    within = loc_obs % 512
    places = (slab // 2) * 128 + ((slab + here) % 2) * 1024 + within % 128
    places = places.reshape(CHUNKS * LOC)
    code = (within // 128) * 16 + loc_level
    (weights,) = call(weight_kernel, [(CHUNKS * LOC, 128)], [VMEM])(code)
    place = (obs_comp * (depth * height) + obs_cell // extent).reshape(1, 512)
    lane = (obs_cell % extent).reshape(1, 512)
    level = ((obs_cell // extent) % height).astype(F32).reshape(1, 512)
    core = here & 1
    value = lax.dynamic_index_in_dim(obs_value.reshape(parts // 2, 2, 4, 128), core, 1, keepdims=False)
    value = value.reshape(K, 128)
    precision = lax.dynamic_index_in_dim(obs_precision.reshape(parts // 2, 2, 4, 128), core, 1, keepdims=False)
    precision = precision.reshape(K, 128)

    (own,) = call(copy_kernel, [field.shape], [pl.BlockSpec(memory_space=pl.ANY)])(field)
    before = lax.ppermute(field, "space", up)
    after = lax.ppermute(field, "space", down)
    message, terms = call(
        model_kernel, [(parts * LINES, 128), (3, 3 * depth * height, extent)], [VMEM] * 6
    )(before, own, after, place, lane, level)
    message = lax.all_to_all(message.reshape(parts, LINES, extent), "space", 0, 0, tiled=True)
    message = message.reshape(parts * LINES, extent)
    (send,) = call(
        functools.partial(forecast_kernel, depth * parts * extent),
        [(K * ROWS, 128)],
        [SMEM] + [VMEM] * 3,
        [pltpu.VMEM((3 * depth * height, extent), F32)],
    )(core.reshape(1), message, own, terms)
    received = exchange(send, "member", K)
    (near,) = call(table_kernel, [(parts * 64, 128)], [VMEM] * 3)(received, value, precision)
    far = lax.ppermute(near, "space", [(i, i ^ 1) for i in range(parts)])
    tiles, centres = call(spread_kernel, [(4, 256, 576), (9, 128)], [VMEM], kinds=[BF16, F32])(received)
    (result,) = call(
        analysis_kernel, [(K * BACK, 128)], [SMEM] + [VMEM] * 5, SCRATCH, 32 * 2**20
    )(places, weights, near, far, tiles, centres)
    returned = exchange(result, "member", K)
    (result,) = call(order_kernel, [(3, depth, height, extent)], [VMEM])(returned)
    return result[None]


def solution(mesh):
    in_specs = (
        P("member", None, "space", None, None),
        P("space"),
        P("space"),
        P(),
        P(),
        P(("space", "member"), None),
        P(("space", "member"), None),
    )
    out_specs = P("member", None, "space", None, None)
    return jax.shard_map(shards, mesh=mesh, in_specs=in_specs, out_specs=out_specs, check_vma=False)
```

```python
import functools

import jax
import jax.numpy as jnp
from jax import lax
from jax.experimental import pallas as pl
from jax.experimental.pallas import tpu as pltpu
from jax.sharding import PartitionSpec as P

NS_ITERS = 8
LEVELS = 8
K = 32
LOC = 128
CHUNKS = 32
ROWS = 41
LINES = 24
BACK = 9

PAIRS = ((0, 0), (1, 1), (2, 2), (0, 1), (0, 2), (1, 2))
F32 = jnp.float32
BF16 = jnp.bfloat16
VMEM = pl.BlockSpec(memory_space=pltpu.VMEM)
SMEM = pl.BlockSpec(memory_space=pltpu.SMEM)


def iota(shape, dim):
    return lax.broadcasted_iota(jnp.int32, shape, dim)


def pair_index(first, second):
    return PAIRS.index((min(first, second), max(first, second)))


def split2(value):
    high = value.astype(BF16)
    return high, (value - high.astype(F32)).astype(BF16)


def split3(value):
    high = value.astype(BF16)
    rest = value - high.astype(F32)
    middle = rest.astype(BF16)
    return high, middle, (rest - middle.astype(F32)).astype(BF16)


def dot(left, right):
    return jnp.dot(left, right, preferred_element_type=F32)


def dot_t(left, right):
    return lax.dot_general(left, right, (((0,), (0,)), ((), ())), preferred_element_type=F32)


def along_y(plane):
    count = plane.shape[0]
    row = iota(plane.shape, 0)
    later = jnp.where(row == count - 1, 0.0, pltpu.roll(plane, count - 1, 0))
    earlier = jnp.where(row == 0, 0.0, pltpu.roll(plane, 1, 0))
    return 0.5 * (later - earlier)


def along_z(plane):
    count = plane.shape[1]
    return 0.5 * (pltpu.roll(plane, count - 1, 1) - pltpu.roll(plane, 1, 1))


def filter_z(plane):
    count = plane.shape[1]
    return 0.25 * (pltpu.roll(plane, 1, 1) + 2.0 * plane + pltpu.roll(plane, count - 1, 1))


def filter_xz(planes, p):
    return filter_z(0.25 * (planes[p - 1] + 2.0 * planes[p] + planes[p + 1]))


def strain(fields, p):
    grads = []
    for b in range(3):
        if b == 0:
            grads.append([0.5 * (f[p + 1] - f[p - 1]) for f in fields])
        elif b == 1:
            grads.append([along_y(f[p]) for f in fields])
        else:
            grads.append([along_z(f[p]) for f in fields])
    return [0.5 * (grads[b][a] + grads[a][b]) for a, b in PAIRS]


def weighted(terms):
    return terms[0] + terms[1] + terms[2] + 2.0 * (terms[3] + terms[4] + terms[5])


def magnitude(rate):
    return jnp.sqrt(2.0 * weighted([r * r for r in rate]))


def shifted_y(plane, step):
    count = plane.shape[0]
    row = iota(plane.shape, 0)
    if step > 0:
        return jnp.where(row == count - 1, 0.0, pltpu.roll(plane, count - 1, 0))
    return jnp.where(row == 0, 0.0, pltpu.roll(plane, 1, 0))


def pick(pieces, choice, spot):
    picked = dot_t(pieces[-1], choice)
    for piece in pieces[-2::-1]:
        picked = picked + dot_t(piece, choice)
    return jnp.sum(jnp.where(spot, picked, 0.0), axis=0, keepdims=True)


def first_kernel(source, cell, comp, own, chosen, ready):
    pltpu.sync_copy(source, own)
    level = cell[...] >> 7
    place = comp[...] * 96 + level
    choice = (iota((288, 512), 0) == place).astype(F32).astype(BF16)
    chosen[...] = choice
    spot = iota((128, 512), 0) == (cell[...] & 127)
    flow = pick(split3(own[...].reshape(288, 128)), choice, spot)
    level = jnp.where(level >= 48, level - 48, level).astype(F32)
    ready[...] = jnp.concatenate([flow, level, jnp.zeros((6, 512), F32)], axis=0)


def model_kernel(before, own, after, cell, chosen, ready, message, terms):
    fields = [
        {0: before[a, 0], 1: before[a, 1], 2: own[a, 0], 3: own[a, 1], 4: after[a, 0], 5: after[a, 1]}
        for a in range(3)
    ]
    tau = [{} for _ in PAIRS]
    for p in range(1, 5):
        rate = strain(fields, p)
        size = magnitude(rate)
        for i in range(6):
            tau[i][p] = size * rate[i]
    for a in range(3):
        for x in range(2):
            p = x + 2
            start = a * 96 + x * 48
            along = tau[pair_index(a, 0)]
            flat = 0.5 * (along[p + 1] - along[p - 1]) + along_z(tau[pair_index(a, 2)][p])
            upright = 0.25 * tau[pair_index(a, 1)][p]
            terms[0, start : start + 48, :] = 0.5 * flat
            terms[1, start : start + 48, :] = shifted_y(upright, 1)
            terms[2, start : start + 48, :] = -shifted_y(upright, -1)
    choice = chosen[...]
    spot = iota((128, 512), 0) == (cell[...] & 127)
    lines = [ready[0:1, :]]
    for f in range(3):
        lines.append(pick(split2(terms[f]), choice, spot))
    lines.append(ready[1:2, :])
    smooth = [{p: filter_xz(f, p) for p in range(1, 5)} for f in fields]
    numer = 0.0
    denom = 0.0
    for p in (2, 3):
        rate = strain(smooth, p)
        size = magnitude(rate)
        top, bottom = [], []
        for i, (a, b) in enumerate(PAIRS):
            product = {q: fields[a][q] * fields[b][q] for q in (p - 1, p, p + 1)}
            leonard = filter_xz(product, p) - smooth[a][p] * smooth[b][p]
            model = 2.0 * (filter_xz(tau[i], p) - 4.0 * size * rate[i])
            top.append(leonard * model)
            bottom.append(model * model)
        numer = numer + weighted(top)
        denom = denom + weighted(bottom)
    pad = jnp.zeros((32, 128), F32)
    both = jnp.concatenate([numer, denom, pad], axis=0).T
    total = jnp.sum(both, axis=0, keepdims=True)
    rows = [line[:, q * 128 : (q + 1) * 128] for line in lines for q in range(4)]
    block = jnp.concatenate(rows + [total, jnp.zeros((3, 128), F32)], axis=0)
    for i in range(message.shape[0] // LINES):
        message[i * LINES : (i + 1) * LINES, :] = block


def forecast_kernel(count, core, message, own, terms, send, state):
    parts = message.shape[0] // LINES
    total = jnp.sum(message[pl.ds(20, parts, stride=LINES), :], axis=0, keepdims=True)
    denom = pltpu.roll(total, 128 - 48, 1)
    coeff = (total / count) / (denom / count + 1e-6)
    coeff = jnp.where(iota((1, 128), 1) < 48, coeff, 0.0)
    column = jnp.broadcast_to(coeff, (128, 128)).T[:48]
    upper = shifted_y(column, 1)
    lower = shifted_y(column, -1)
    for a in range(3):
        for x in range(2):
            start = a * 96 + x * 48
            end = start + 48
            change = column * terms[0, start:end, :]
            change = change + (upper * terms[1, start:end, :] + lower * terms[2, start:end, :])
            state[start:end, :] = own[a, x] + change
    odd = core[0] == 1
    flow, height = [], []

    def lines(f):
        pieces = []
        for i in range(parts // 2):
            even_at = 2 * i * LINES + 4 * f
            odd_at = even_at + LINES
            pieces.append(jnp.where(odd, message[odd_at : odd_at + 4, :], message[even_at : even_at + 4, :]))
        return jnp.concatenate(pieces, axis=0)

    height = lines(4).astype(jnp.int32)
    table = jnp.broadcast_to(coeff, height.shape)

    def look(where):
        where = jnp.clip(where, 0, 127)
        return jnp.take_along_axis(table, where, axis=1)

    seen = lines(0) + look(height) * lines(1)
    seen = seen + (look(height + 1) * lines(2) + look(height - 1) * lines(3))
    for m in range(K):
        base = m * ROWS
        for a in range(3):
            send[base + 3 * a : base + 3 * a + 3, :] = state[a * 96 + 3 * m : a * 96 + 3 * m + 3, :]
        send[base + 9 : base + ROWS, :] = seen


def table_kernel(received, value, precision, table):
    member = iota((K, 128), 0)
    for i in range(8):
        parts = []
        for q in range(4):
            r = 4 * i + q
            seen = received[pl.ds(9 + r, K, stride=ROWS), :]
            mean = jnp.sum(seen, axis=0, keepdims=True) * (1.0 / K)
            innov = value[r : r + 1, :] - mean
            root = jnp.sqrt(precision[r : r + 1, :])
            parts.append(jnp.where(member == K - 1, innov, seen - mean) * root)
        table[i * 128 : (i + 1) * 128, :] = jnp.concatenate(parts, axis=0).T


def block_diagonal(value, mask):
    return jnp.concatenate([value] * 8, axis=0) * mask


def times_blocks(left, right, mask):
    r1, r2 = split2(right)
    l1, l2 = split2(left)
    rows = left.shape[0]
    wide = dot(jnp.concatenate([l1, l2], axis=0), block_diagonal(r1, mask))
    return wide[:rows] + wide[rows:] + dot(l1, block_diagonal(r2, mask))


def exact_times(left, constant):
    rows = left.shape[0]
    wide = dot(jnp.concatenate(split3(left), axis=0), constant)
    return (wide[2 * rows :] + wide[rows : 2 * rows]) + wide[:rows]


def weight_kernel(code, weights):
    columns = jnp.concatenate([code[...], jnp.zeros((96, 128), jnp.int32)], axis=0).T
    quarter = iota((LOC, 128), 1) // 32
    for c in range(CHUNKS):
        mark = jnp.broadcast_to(columns[:, c : c + 1], (LOC, 128))
        level = jnp.sqrt((mark & 15).astype(F32) * (1.0 / LEVELS))
        weights[c * LOC : (c + 1) * LOC, :] = jnp.where((mark >> 4) == quarter, level, 0.0)


def spread_kernel(received, tiles, centres):
    cells = [received[pl.ds(r, K, stride=ROWS), :] for r in range(9)]
    means = [jnp.sum(v, axis=0, keepdims=True) * (1.0 / K) for v in cells]
    centres[...] = jnp.concatenate(means, axis=0)
    spreads = [v - m for v, m in zip(cells, means)]
    owner = iota((256, 288), 0) // 32
    chunk = (iota((256, 288), 1) % 32) // 4
    here = jnp.where(chunk == owner, 1.0, 0.0).astype(BF16)
    for g in range(4):
        packed = jnp.concatenate([v[:, 32 * g : 32 * g + 32] for v in spreads], axis=1)
        h1, h2 = split2(packed)
        tiles[g, :, 0:288] = block_diagonal(h1, here)
        tiles[g, :, 288:576] = block_diagonal(h2, here)


def folded(rows, weights):
    lone = rows * weights
    lone = lone + pltpu.roll(lone, 64, 1)
    return lone + pltpu.roll(lone, 32, 1)


def four_gram(pack):
    quarter = iota((LOC, 128), 1) // 32
    high, low = split2(pack)
    blocks = [jnp.where(quarter == i, 1.0, 0.0).astype(BF16) for i in range(4)]
    right1 = jnp.concatenate([high * b for b in blocks], axis=0)
    right2 = jnp.concatenate([low * b for b in blocks], axis=0)
    turned = pack.T
    turned = jnp.concatenate([turned[32 * i : 32 * i + 32] for i in range(4)], axis=1)
    left1, left2 = split2(turned)
    wide = dot(jnp.concatenate([left1, left2], axis=0), right1)
    return (wide[K:] + dot(left1, right2)) + wide[:K]


def analysis_kernel(places, weights, near, far, tiles, centres, out, table, picked):
    table[0:1024, :] = near[...]
    table[1024:2048, :] = far[...]

    quarter = iota((LOC, 128), 1) // 32

    def fetch(four, carry):
        base = pl.multiple_of(four * (4 * LOC), 4 * LOC)
        target = picked.at[pl.ds(base, 4 * LOC)]
        for j in range(4 * LOC):
            target[j : j + 1, :] = table[pl.ds(places[base + j], 1), :]
        return carry

    lax.fori_loop(0, CHUNKS // 4, fetch, 0)
    grams = []
    for four in range(CHUNKS // 4):
        pack = None
        for i in range(4):
            at = (4 * four + i) * LOC
            lone = folded(picked[at : at + LOC, :], weights[at : at + LOC, :])
            pack = lone if i == 0 else jnp.where(quarter == i, lone, pack)
        grams.append(four_gram(pack))
    packs = [jnp.concatenate([grams[2 * g], grams[2 * g + 1]], axis=1) for g in range(4)]

    tall = iota((256, 256), 0)
    wide_lane = iota((256, 256), 1)
    same = (tall // 32) == (wide_lane // 32)
    mask = jnp.where(same, 1.0, 0.0).astype(BF16)
    last = (wide_lane % 32) == 31
    not_last_row = (tall % 32) != 31
    rebuild = jnp.where(last, jnp.where(same & not_last_row, -1.0, 0.0), jnp.where(tall == wide_lane, 1.0, 0.0))
    rebuild = rebuild.astype(BF16)
    member = iota((K, 256), 0)
    eye = jnp.where(member == iota((K, 256), 1) % 32, 1.0, 0.0)

    count = len(packs)
    drive, scale, y, z = [], [], [], []
    for g in range(count):
        pack = packs[g]
        body = jnp.where(member == K - 1, 0.0, pack)
        body = jnp.where(member == K - 1, -jnp.sum(body, axis=0, keepdims=True), body)
        push = jnp.broadcast_to(pack[K - 1 : K, :], (16, 256))
        whole = exact_times(jnp.concatenate([body, push], axis=0), rebuild)
        matrix = whole[:K] + ((K - 1) / 1.1) * eye
        drive.append(whole[K:])
        square = jnp.broadcast_to(jnp.sum(matrix * matrix, axis=0, keepdims=True), (16, 256))
        norm = jnp.sqrt(exact_times(square, mask))
        scale.append(norm)
        y.append(matrix / norm[0:1])
    for sweep in range(NS_ITERS):
        for g in range(count):
            if sweep == 0:
                factor = 1.5 * eye - 0.5 * y[g]
                both = times_blocks(jnp.concatenate([y[g], drive[g]], axis=0), factor, mask)
                y[g], drive[g] = both[:K], both[K:]
                z.append(factor)
                continue
            factor = 1.5 * eye - 0.5 * times_blocks(z[g], y[g], mask)
            if sweep == NS_ITERS - 1:
                both = times_blocks(jnp.concatenate([z[g], drive[g]], axis=0), factor, mask)
                z[g], drive[g] = both[:K], both[K:]
            else:
                both = times_blocks(jnp.concatenate([y[g], z[g], drive[g]], axis=0), factor, mask)
                y[g], z[g], drive[g] = both[:K], both[K : 2 * K], both[2 * K :]
    moved = []
    for g in range(count):
        pull = times_blocks(drive[g], z[g], mask) / scale[g]
        root = z[g] * (jnp.sqrt(float(K - 1)) / jnp.sqrt(scale[g][0:1]))
        left1, left2 = split2(jnp.concatenate([root, pull], axis=0))
        rows = left1.shape[0]
        part = dot(jnp.concatenate([left1, left2], axis=0), tiles[g])
        part = part[:rows, :288] + part[rows:, :288] + part[:rows, 288:]
        moved.append(part[:K] + part[K : K + 1])
    for r in range(9):
        row = jnp.concatenate([part[:, 32 * r : 32 * r + 32] for part in moved], axis=1)
        out[pl.ds(r, K, stride=BACK), :] = row + centres[r : r + 1, :]


SCRATCH = [pltpu.VMEM((2048, 128), F32), pltpu.VMEM((CHUNKS * LOC, 128), F32)]


def order_kernel(returned, out):
    for m in range(K):
        x, y = m // 16, 3 * (m % 16)
        for a in range(3):
            out[a, x, y : y + 3, :] = returned[m * BACK + 3 * a : m * BACK + 3 * a + 3, :]


def call(kernel, shapes, ins, scratch=(), limit=24 * 2**20, kinds=None):
    return pl.pallas_call(
        kernel,
        out_shape=[jax.ShapeDtypeStruct(s, t) for s, t in zip(shapes, kinds or [F32] * len(shapes))],
        in_specs=ins,
        out_specs=[VMEM] * len(shapes),
        scratch_shapes=list(scratch),
        compiler_params=pltpu.CompilerParams(vmem_limit_bytes=limit),
    )


def exchange(rows, axis, count):
    width = rows.size // count
    sent = lax.all_to_all(rows.reshape(count, 1, width), axis, 0, 0, tiled=True)
    return sent.reshape(rows.shape)


def shards(ensemble, obs_cell, obs_comp, obs_value, obs_precision, loc_obs, loc_level):
    field = ensemble[0]
    _, depth, height, extent = field.shape
    parts = lax.axis_size("space")
    here = lax.axis_index("space")
    up = [(i, (i + 1) % parts) for i in range(parts)]
    down = [(j, i) for i, j in up]

    slab = loc_obs // 512
    within = loc_obs % 512
    places = (slab // 2) * 128 + ((slab + here) % 2) * 1024 + within % 128
    places = places.reshape(CHUNKS * LOC)
    code = (within // 128) * 16 + loc_level
    core = here & 1
    value = lax.dynamic_index_in_dim(obs_value.reshape(parts // 2, 2, 4, 128), core, 1, keepdims=False)
    value = value.reshape(K, 128)
    precision = lax.dynamic_index_in_dim(obs_precision.reshape(parts // 2, 2, 4, 128), core, 1, keepdims=False)
    precision = precision.reshape(K, 128)

    cell = obs_cell.reshape(1, 512)
    own, chosen, ready = call(
        first_kernel,
        [field.shape, (3 * depth * height, 512), (8, 512)],
        [pl.BlockSpec(memory_space=pl.ANY), VMEM, VMEM],
        kinds=[F32, BF16, F32],
    )(field, cell, obs_comp.reshape(1, 512))
    before = lax.ppermute(field, "space", up)
    after = lax.ppermute(field, "space", down)
    message, terms = call(
        model_kernel, [(parts * LINES, 128), (3, 3 * depth * height, extent)], [VMEM] * 6
    )(before, own, after, cell, chosen, ready)
    message = lax.all_to_all(message.reshape(parts, LINES, extent), "space", 0, 0, tiled=True)
    (weights,) = call(weight_kernel, [(CHUNKS * LOC, 128)], [VMEM])(code)
    message, weights, places = lax.optimization_barrier((message, weights, places))
    message = message.reshape(parts * LINES, extent)
    (send,) = call(
        functools.partial(forecast_kernel, depth * parts * extent),
        [(K * ROWS, 128)],
        [SMEM] + [VMEM] * 3,
        [pltpu.VMEM((3 * depth * height, extent), F32)],
    )(core.reshape(1), message, own, terms)
    received = exchange(send, "member", K)
    (near,) = call(table_kernel, [(parts * 64, 128)], [VMEM] * 3)(received, value, precision)
    far = lax.ppermute(near, "space", [(i, i ^ 1) for i in range(parts)])
    tiles, centres = call(spread_kernel, [(4, 256, 576), (9, 128)], [VMEM], kinds=[BF16, F32])(received)
    (result,) = call(
        analysis_kernel, [(K * BACK, 128)], [SMEM] + [VMEM] * 5, SCRATCH, 32 * 2**20
    )(places, weights, near, far, tiles, centres)
    returned = exchange(result, "member", K)
    (result,) = call(order_kernel, [(3, depth, height, extent)], [VMEM])(returned)
    return result[None]


def solution(mesh):
    in_specs = (
        P("member", None, "space", None, None),
        P("space"),
        P("space"),
        P(),
        P(),
        P(("space", "member"), None),
        P(("space", "member"), None),
    )
    out_specs = P("member", None, "space", None, None)
    return jax.shard_map(shards, mesh=mesh, in_specs=in_specs, out_specs=out_specs, check_vma=False)
```

```python
import functools

import jax
import jax.numpy as jnp
from jax import lax
from jax.experimental import pallas as pl
from jax.experimental.pallas import tpu as pltpu
from jax.sharding import PartitionSpec as P

NS_ITERS = 8
LEVELS = 8
K = 32
LOC = 128
CHUNKS = 32
ROWS = 41
LINES = 24
BACK = 9

PAIRS = ((0, 0), (1, 1), (2, 2), (0, 1), (0, 2), (1, 2))
F32 = jnp.float32
BF16 = jnp.bfloat16
VMEM = pl.BlockSpec(memory_space=pltpu.VMEM)
SMEM = pl.BlockSpec(memory_space=pltpu.SMEM)


def iota(shape, dim):
    return lax.broadcasted_iota(jnp.int32, shape, dim)


def pair_index(first, second):
    return PAIRS.index((min(first, second), max(first, second)))


def split2(value):
    high = value.astype(BF16)
    return high, (value - high.astype(F32)).astype(BF16)


def split3(value):
    high = value.astype(BF16)
    rest = value - high.astype(F32)
    middle = rest.astype(BF16)
    return high, middle, (rest - middle.astype(F32)).astype(BF16)


def dot(left, right):
    return jnp.dot(left, right, preferred_element_type=F32)


def dot_t(left, right):
    return lax.dot_general(left, right, (((0,), (0,)), ((), ())), preferred_element_type=F32)


def along_y(plane):
    count = plane.shape[0]
    row = iota(plane.shape, 0)
    later = jnp.where(row == count - 1, 0.0, pltpu.roll(plane, count - 1, 0))
    earlier = jnp.where(row == 0, 0.0, pltpu.roll(plane, 1, 0))
    return 0.5 * (later - earlier)


def along_z(plane):
    count = plane.shape[1]
    return 0.5 * (pltpu.roll(plane, count - 1, 1) - pltpu.roll(plane, 1, 1))


def filter_z(plane):
    count = plane.shape[1]
    return 0.25 * (pltpu.roll(plane, 1, 1) + 2.0 * plane + pltpu.roll(plane, count - 1, 1))


def filter_xz(planes, p):
    return filter_z(0.25 * (planes[p - 1] + 2.0 * planes[p] + planes[p + 1]))


def strain(fields, p):
    grads = []
    for b in range(3):
        if b == 0:
            grads.append([0.5 * (f[p + 1] - f[p - 1]) for f in fields])
        elif b == 1:
            grads.append([along_y(f[p]) for f in fields])
        else:
            grads.append([along_z(f[p]) for f in fields])
    return [0.5 * (grads[b][a] + grads[a][b]) for a, b in PAIRS]


def weighted(terms):
    return terms[0] + terms[1] + terms[2] + 2.0 * (terms[3] + terms[4] + terms[5])


def magnitude(rate):
    return jnp.sqrt(2.0 * weighted([r * r for r in rate]))


def shifted_y(plane, step):
    count = plane.shape[0]
    row = iota(plane.shape, 0)
    if step > 0:
        return jnp.where(row == count - 1, 0.0, pltpu.roll(plane, count - 1, 0))
    return jnp.where(row == 0, 0.0, pltpu.roll(plane, 1, 0))


def pick(pieces, choice, spot):
    picked = dot_t(pieces[-1], choice)
    for piece in pieces[-2::-1]:
        picked = picked + dot_t(piece, choice)
    return jnp.sum(jnp.where(spot, picked, 0.0), axis=0, keepdims=True)


def first_kernel(source, cell, comp, own, chosen, ready):
    pltpu.sync_copy(source, own)
    level = cell[...] >> 7
    place = comp[...] * 96 + level
    choice = (iota((288, 512), 0) == place).astype(F32).astype(BF16)
    chosen[...] = choice
    spot = iota((128, 512), 0) == (cell[...] & 127)
    flow = pick(split3(own[...].reshape(288, 128)), choice, spot)
    level = jnp.where(level >= 48, level - 48, level).astype(F32)
    ready[...] = jnp.concatenate([flow, level, jnp.zeros((6, 512), F32)], axis=0)


def model_kernel(before, own, after, cell, chosen, ready, message, terms):
    fields = [
        {0: before[a, 0], 1: before[a, 1], 2: own[a, 0], 3: own[a, 1], 4: after[a, 0], 5: after[a, 1]}
        for a in range(3)
    ]
    tau = [{} for _ in PAIRS]
    for p in range(1, 5):
        rate = strain(fields, p)
        size = magnitude(rate)
        for i in range(6):
            tau[i][p] = size * rate[i]
    for a in range(3):
        for x in range(2):
            p = x + 2
            start = a * 96 + x * 48
            along = tau[pair_index(a, 0)]
            flat = 0.5 * (along[p + 1] - along[p - 1]) + along_z(tau[pair_index(a, 2)][p])
            upright = 0.25 * tau[pair_index(a, 1)][p]
            terms[0, start : start + 48, :] = 0.5 * flat
            terms[1, start : start + 48, :] = shifted_y(upright, 1)
            terms[2, start : start + 48, :] = -shifted_y(upright, -1)
    choice = chosen[...]
    spot = iota((128, 512), 0) == (cell[...] & 127)
    lines = [ready[0:1, :]]
    for f in range(3):
        lines.append(pick(split2(terms[f]), choice, spot))
    lines.append(ready[1:2, :])
    smooth = [{p: filter_xz(f, p) for p in range(1, 5)} for f in fields]
    numer = 0.0
    denom = 0.0
    for p in (2, 3):
        rate = strain(smooth, p)
        size = magnitude(rate)
        top, bottom = [], []
        for i, (a, b) in enumerate(PAIRS):
            product = {q: fields[a][q] * fields[b][q] for q in (p - 1, p, p + 1)}
            leonard = filter_xz(product, p) - smooth[a][p] * smooth[b][p]
            model = 2.0 * (filter_xz(tau[i], p) - 4.0 * size * rate[i])
            top.append(leonard * model)
            bottom.append(model * model)
        numer = numer + weighted(top)
        denom = denom + weighted(bottom)
    pad = jnp.zeros((32, 128), F32)
    both = jnp.concatenate([numer, denom, pad], axis=0).T
    total = jnp.sum(both, axis=0, keepdims=True)
    rows = [line[:, q * 128 : (q + 1) * 128] for line in lines for q in range(4)]
    block = jnp.concatenate(rows + [total, jnp.zeros((3, 128), F32)], axis=0)
    for i in range(message.shape[0] // LINES):
        message[i * LINES : (i + 1) * LINES, :] = block


def forecast_kernel(count, core, message, own, terms, send, state):
    parts = message.shape[0] // LINES
    total = jnp.sum(message[pl.ds(20, parts, stride=LINES), :], axis=0, keepdims=True)
    denom = pltpu.roll(total, 128 - 48, 1)
    coeff = (total / count) / (denom / count + 1e-6)
    coeff = jnp.where(iota((1, 128), 1) < 48, coeff, 0.0)
    column = jnp.broadcast_to(coeff, (128, 128)).T[:48]
    upper = shifted_y(column, 1)
    lower = shifted_y(column, -1)
    for a in range(3):
        for x in range(2):
            start = a * 96 + x * 48
            end = start + 48
            change = column * terms[0, start:end, :]
            change = change + (upper * terms[1, start:end, :] + lower * terms[2, start:end, :])
            state[start:end, :] = own[a, x] + change
    odd = core[0] == 1
    flow, height = [], []

    def lines(f):
        pieces = []
        for i in range(parts // 2):
            even_at = 2 * i * LINES + 4 * f
            odd_at = even_at + LINES
            pieces.append(jnp.where(odd, message[odd_at : odd_at + 4, :], message[even_at : even_at + 4, :]))
        return jnp.concatenate(pieces, axis=0)

    height = lines(4).astype(jnp.int32)
    table = jnp.broadcast_to(coeff, height.shape)

    def look(where):
        where = jnp.clip(where, 0, 127)
        return jnp.take_along_axis(table, where, axis=1)

    seen = lines(0) + look(height) * lines(1)
    seen = seen + (look(height + 1) * lines(2) + look(height - 1) * lines(3))
    for m in range(K):
        base = m * ROWS
        for a in range(3):
            send[base + 3 * a : base + 3 * a + 3, :] = state[a * 96 + 3 * m : a * 96 + 3 * m + 3, :]
        send[base + 9 : base + ROWS, :] = seen


def table_kernel(received, value, precision, table):
    member = iota((K, 128), 0)
    for i in range(8):
        parts = []
        for q in range(4):
            r = 4 * i + q
            seen = received[pl.ds(9 + r, K, stride=ROWS), :]
            mean = jnp.sum(seen, axis=0, keepdims=True) * (1.0 / K)
            innov = value[r : r + 1, :] - mean
            root = jnp.sqrt(precision[r : r + 1, :])
            parts.append(jnp.where(member == K - 1, innov, seen - mean) * root)
        table[i * 128 : (i + 1) * 128, :] = jnp.concatenate(parts, axis=0).T


def block_diagonal(value, mask):
    return jnp.concatenate([value] * 8, axis=0) * mask


def times_blocks(left, right, mask):
    r1, r2 = split2(right)
    l1, l2 = split2(left)
    rows = left.shape[0]
    wide = dot(jnp.concatenate([l1, l2], axis=0), block_diagonal(r1, mask))
    return wide[:rows] + wide[rows:] + dot(l1, block_diagonal(r2, mask))


def exact_times(left, constant):
    rows = left.shape[0]
    wide = dot(jnp.concatenate(split3(left), axis=0), constant)
    return (wide[2 * rows :] + wide[rows : 2 * rows]) + wide[:rows]


def weight_kernel(code, weights):
    columns = jnp.concatenate([code[...], jnp.zeros((96, 128), jnp.int32)], axis=0).T
    quarter = iota((LOC, 128), 1) // 32
    for c in range(CHUNKS):
        mark = jnp.broadcast_to(columns[:, c : c + 1], (LOC, 128))
        level = jnp.sqrt((mark & 15).astype(F32) * (1.0 / LEVELS))
        weights[c * LOC : (c + 1) * LOC, :] = jnp.where((mark >> 4) == quarter, level, 0.0)


def spread_kernel(received, tiles, centres, masks):
    tall = iota((256, 256), 0)
    wide_lane = iota((256, 256), 1)
    same = (tall // 32) == (wide_lane // 32)
    mask = jnp.where(same, 1.0, 0.0).astype(BF16)
    last = (wide_lane % 32) == 31
    not_last_row = (tall % 32) != 31
    rebuild = jnp.where(last, jnp.where(same & not_last_row, -1.0, 0.0), jnp.where(tall == wide_lane, 1.0, 0.0))
    masks[0] = mask
    masks[1] = rebuild.astype(BF16)
    cells = [received[pl.ds(r, K, stride=ROWS), :] for r in range(9)]
    means = [jnp.sum(v, axis=0, keepdims=True) * (1.0 / K) for v in cells]
    centres[...] = jnp.concatenate(means, axis=0)
    spreads = [v - m for v, m in zip(cells, means)]
    owner = iota((256, 288), 0) // 32
    chunk = (iota((256, 288), 1) % 32) // 4
    here = jnp.where(chunk == owner, 1.0, 0.0).astype(BF16)
    for g in range(4):
        packed = jnp.concatenate([v[:, 32 * g : 32 * g + 32] for v in spreads], axis=1)
        h1, h2 = split2(packed)
        tiles[g, :, 0:288] = block_diagonal(h1, here)
        tiles[g, :, 288:576] = block_diagonal(h2, here)


def folded(rows, weights):
    lone = rows * weights
    lone = lone + pltpu.roll(lone, 64, 1)
    return lone + pltpu.roll(lone, 32, 1)


def four_gram(pack):
    quarter = iota((LOC, 128), 1) // 32
    high, low = split2(pack)
    blocks = [jnp.where(quarter == i, 1.0, 0.0).astype(BF16) for i in range(4)]
    right1 = jnp.concatenate([high * b for b in blocks], axis=0)
    right2 = jnp.concatenate([low * b for b in blocks], axis=0)
    turned = pack.T
    turned = jnp.concatenate([turned[32 * i : 32 * i + 32] for i in range(4)], axis=1)
    left1, left2 = split2(turned)
    wide = dot(jnp.concatenate([left1, left2], axis=0), right1)
    return (wide[K:] + dot(left1, right2)) + wide[:K]


def analysis_kernel(places, weights, near, far, tiles, centres, masks, out, table, picked):
    table[0:1024, :] = near[...]
    table[1024:2048, :] = far[...]

    quarter = iota((LOC, 128), 1) // 32

    def fetch(at, carry):
        picked[pl.ds(at, 1), :] = table[pl.ds(places[at], 1), :]
        return carry

    lax.fori_loop(0, CHUNKS * LOC, fetch, 0, unroll=True)
    grams = []
    for four in range(CHUNKS // 4):
        pack = None
        for i in range(4):
            at = (4 * four + i) * LOC
            lone = folded(picked[at : at + LOC, :], weights[at : at + LOC, :])
            pack = lone if i == 0 else jnp.where(quarter == i, lone, pack)
        grams.append(four_gram(pack))
    packs = [jnp.concatenate([grams[2 * g], grams[2 * g + 1]], axis=1) for g in range(4)]

    mask = masks[0]
    rebuild = masks[1]
    member = iota((K, 256), 0)
    eye = jnp.where(member == iota((K, 256), 1) % 32, 1.0, 0.0)

    count = len(packs)
    drive, scale, y, z = [], [], [], []
    for g in range(count):
        pack = packs[g]
        body = jnp.where(member == K - 1, 0.0, pack)
        body = jnp.where(member == K - 1, -jnp.sum(body, axis=0, keepdims=True), body)
        push = jnp.broadcast_to(pack[K - 1 : K, :], (16, 256))
        whole = exact_times(jnp.concatenate([body, push], axis=0), rebuild)
        matrix = whole[:K] + ((K - 1) / 1.1) * eye
        drive.append(whole[K:])
        square = jnp.broadcast_to(jnp.sum(matrix * matrix, axis=0, keepdims=True), (16, 256))
        norm = jnp.sqrt(exact_times(square, mask))
        scale.append(norm)
        y.append(matrix / norm[0:1])
    for sweep in range(NS_ITERS):
        for g in range(count):
            if sweep == 0:
                factor = 1.5 * eye - 0.5 * y[g]
                both = times_blocks(jnp.concatenate([y[g], drive[g]], axis=0), factor, mask)
                y[g], drive[g] = both[:K], both[K:]
                z.append(factor)
                continue
            factor = 1.5 * eye - 0.5 * times_blocks(z[g], y[g], mask)
            if sweep == NS_ITERS - 1:
                both = times_blocks(jnp.concatenate([z[g], drive[g]], axis=0), factor, mask)
                z[g], drive[g] = both[:K], both[K:]
            else:
                both = times_blocks(jnp.concatenate([y[g], z[g], drive[g]], axis=0), factor, mask)
                y[g], z[g], drive[g] = both[:K], both[K : 2 * K], both[2 * K :]
    moved = []
    for g in range(count):
        pull = times_blocks(drive[g], z[g], mask) / scale[g]
        root = z[g] * (jnp.sqrt(float(K - 1)) / jnp.sqrt(scale[g][0:1]))
        left1, left2 = split2(jnp.concatenate([root, pull], axis=0))
        rows = left1.shape[0]
        part = dot(jnp.concatenate([left1, left2], axis=0), tiles[g])
        part = part[:rows, :288] + part[rows:, :288] + part[:rows, 288:]
        moved.append(part[:K] + part[K : K + 1])
    for r in range(9):
        row = jnp.concatenate([part[:, 32 * r : 32 * r + 32] for part in moved], axis=1)
        out[pl.ds(r, K, stride=BACK), :] = row + centres[r : r + 1, :]


SCRATCH = [pltpu.VMEM((2048, 128), F32), pltpu.VMEM((CHUNKS * LOC, 128), F32)]


def order_kernel(returned, out):
    for m in range(K):
        x, y = m // 16, 3 * (m % 16)
        for a in range(3):
            out[a, x, y : y + 3, :] = returned[m * BACK + 3 * a : m * BACK + 3 * a + 3, :]


def call(kernel, shapes, ins, scratch=(), limit=24 * 2**20, kinds=None):
    return pl.pallas_call(
        kernel,
        out_shape=[jax.ShapeDtypeStruct(s, t) for s, t in zip(shapes, kinds or [F32] * len(shapes))],
        in_specs=ins,
        out_specs=[VMEM] * len(shapes),
        scratch_shapes=list(scratch),
        compiler_params=pltpu.CompilerParams(vmem_limit_bytes=limit),
    )


def exchange(rows, axis, count):
    width = rows.size // count
    sent = lax.all_to_all(rows.reshape(count, 1, width), axis, 0, 0, tiled=True)
    return sent.reshape(rows.shape)


def shards(ensemble, obs_cell, obs_comp, obs_value, obs_precision, loc_obs, loc_level):
    field = ensemble[0]
    _, depth, height, extent = field.shape
    parts = lax.axis_size("space")
    here = lax.axis_index("space")
    up = [(i, (i + 1) % parts) for i in range(parts)]
    down = [(j, i) for i, j in up]

    slab = loc_obs // 512
    within = loc_obs % 512
    places = (slab // 2) * 128 + ((slab + here) % 2) * 1024 + within % 128
    places = places.reshape(CHUNKS * LOC)
    code = (within // 128) * 16 + loc_level
    core = here & 1
    value = lax.dynamic_index_in_dim(obs_value.reshape(parts // 2, 2, 4, 128), core, 1, keepdims=False)
    value = value.reshape(K, 128)
    precision = lax.dynamic_index_in_dim(obs_precision.reshape(parts // 2, 2, 4, 128), core, 1, keepdims=False)
    precision = precision.reshape(K, 128)

    cell = obs_cell.reshape(1, 512)
    own, chosen, ready = call(
        first_kernel,
        [field.shape, (3 * depth * height, 512), (8, 512)],
        [pl.BlockSpec(memory_space=pl.ANY), VMEM, VMEM],
        kinds=[F32, BF16, F32],
    )(field, cell, obs_comp.reshape(1, 512))
    before = lax.ppermute(field, "space", up)
    after = lax.ppermute(field, "space", down)
    message, terms = call(
        model_kernel, [(parts * LINES, 128), (3, 3 * depth * height, extent)], [VMEM] * 6
    )(before, own, after, cell, chosen, ready)
    message = lax.all_to_all(message.reshape(parts, LINES, extent), "space", 0, 0, tiled=True)
    (weights,) = call(weight_kernel, [(CHUNKS * LOC, 128)], [VMEM])(code)
    message, weights, places = lax.optimization_barrier((message, weights, places))
    message = message.reshape(parts * LINES, extent)
    (send,) = call(
        functools.partial(forecast_kernel, depth * parts * extent),
        [(K * ROWS, 128)],
        [SMEM] + [VMEM] * 3,
        [pltpu.VMEM((3 * depth * height, extent), F32)],
    )(core.reshape(1), message, own, terms)
    received = exchange(send, "member", K)
    (near,) = call(table_kernel, [(parts * 64, 128)], [VMEM] * 3)(received, value, precision)
    far = lax.ppermute(near, "space", [(i, i ^ 1) for i in range(parts)])
    tiles, centres, masks = call(
        spread_kernel, [(4, 256, 576), (9, 128), (2, 256, 256)], [VMEM], kinds=[BF16, F32, BF16]
    )(received)
    (result,) = call(
        analysis_kernel, [(K * BACK, 128)], [SMEM] + [VMEM] * 6, SCRATCH, 32 * 2**20
    )(places, weights, near, far, tiles, centres, masks)
    returned = exchange(result, "member", K)
    (result,) = call(order_kernel, [(3, depth, height, extent)], [VMEM])(returned)
    return result[None]


def solution(mesh):
    in_specs = (
        P("member", None, "space", None, None),
        P("space"),
        P("space"),
        P(),
        P(),
        P(("space", "member"), None),
        P(("space", "member"), None),
    )
    out_specs = P("member", None, "space", None, None)
    return jax.shard_map(shards, mesh=mesh, in_specs=in_specs, out_specs=out_specs, check_vma=False)
```

```python
import functools

import jax
import jax.numpy as jnp
from jax import lax
from jax.experimental import pallas as pl
from jax.experimental.pallas import tpu as pltpu
from jax.sharding import PartitionSpec as P

NS_ITERS = 8
LEVELS = 8
K = 32
LOC = 128
CHUNKS = 32
ROWS = 41
LINES = 24
BACK = 9

PAIRS = ((0, 0), (1, 1), (2, 2), (0, 1), (0, 2), (1, 2))
F32 = jnp.float32
BF16 = jnp.bfloat16
VMEM = pl.BlockSpec(memory_space=pltpu.VMEM)
SMEM = pl.BlockSpec(memory_space=pltpu.SMEM)


def iota(shape, dim):
    return lax.broadcasted_iota(jnp.int32, shape, dim)


def pair_index(first, second):
    return PAIRS.index((min(first, second), max(first, second)))


def split2(value):
    high = value.astype(BF16)
    return high, (value - high.astype(F32)).astype(BF16)


def split3(value):
    high = value.astype(BF16)
    rest = value - high.astype(F32)
    middle = rest.astype(BF16)
    return high, middle, (rest - middle.astype(F32)).astype(BF16)


def dot(left, right):
    return jnp.dot(left, right, preferred_element_type=F32)


def dot_t(left, right):
    return lax.dot_general(left, right, (((0,), (0,)), ((), ())), preferred_element_type=F32)


def along_y(plane):
    count = plane.shape[0]
    row = iota(plane.shape, 0)
    later = jnp.where(row == count - 1, 0.0, pltpu.roll(plane, count - 1, 0))
    earlier = jnp.where(row == 0, 0.0, pltpu.roll(plane, 1, 0))
    return 0.5 * (later - earlier)


def along_z(plane):
    count = plane.shape[1]
    return 0.5 * (pltpu.roll(plane, count - 1, 1) - pltpu.roll(plane, 1, 1))


def filter_z(plane):
    count = plane.shape[1]
    return 0.25 * (pltpu.roll(plane, 1, 1) + 2.0 * plane + pltpu.roll(plane, count - 1, 1))


def filter_xz(planes, p):
    return filter_z(0.25 * (planes[p - 1] + 2.0 * planes[p] + planes[p + 1]))


def strain(fields, p):
    grads = []
    for b in range(3):
        if b == 0:
            grads.append([0.5 * (f[p + 1] - f[p - 1]) for f in fields])
        elif b == 1:
            grads.append([along_y(f[p]) for f in fields])
        else:
            grads.append([along_z(f[p]) for f in fields])
    return [0.5 * (grads[b][a] + grads[a][b]) for a, b in PAIRS]


def weighted(terms):
    return terms[0] + terms[1] + terms[2] + 2.0 * (terms[3] + terms[4] + terms[5])


def magnitude(rate):
    return jnp.sqrt(2.0 * weighted([r * r for r in rate]))


def shifted_y(plane, step):
    count = plane.shape[0]
    row = iota(plane.shape, 0)
    if step > 0:
        return jnp.where(row == count - 1, 0.0, pltpu.roll(plane, count - 1, 0))
    return jnp.where(row == 0, 0.0, pltpu.roll(plane, 1, 0))


def pick(pieces, choice, spot):
    picked = dot_t(pieces[-1], choice)
    for piece in pieces[-2::-1]:
        picked = picked + dot_t(piece, choice)
    return jnp.sum(jnp.where(spot, picked, 0.0), axis=0, keepdims=True)


def first_kernel(source, cell, comp, own, chosen, ready):
    pltpu.sync_copy(source, own)
    level = cell[...] >> 7
    place = comp[...] * 96 + level
    choice = (iota((288, 512), 0) == place).astype(F32).astype(BF16)
    chosen[...] = choice
    spot = iota((128, 512), 0) == (cell[...] & 127)
    flow = pick(split3(own[...].reshape(288, 128)), choice, spot)
    level = jnp.where(level >= 48, level - 48, level).astype(F32)
    ready[...] = jnp.concatenate([flow, level, jnp.zeros((6, 512), F32)], axis=0)


def model_kernel(before, own, after, cell, chosen, ready, message, terms):
    fields = [
        {0: before[a, 0], 1: before[a, 1], 2: own[a, 0], 3: own[a, 1], 4: after[a, 0], 5: after[a, 1]}
        for a in range(3)
    ]
    tau = [{} for _ in PAIRS]
    for p in range(1, 5):
        rate = strain(fields, p)
        size = magnitude(rate)
        for i in range(6):
            tau[i][p] = size * rate[i]
    for a in range(3):
        for x in range(2):
            p = x + 2
            start = a * 96 + x * 48
            along = tau[pair_index(a, 0)]
            flat = 0.5 * (along[p + 1] - along[p - 1]) + along_z(tau[pair_index(a, 2)][p])
            upright = 0.25 * tau[pair_index(a, 1)][p]
            terms[0, start : start + 48, :] = 0.5 * flat
            terms[1, start : start + 48, :] = shifted_y(upright, 1)
            terms[2, start : start + 48, :] = -shifted_y(upright, -1)
    choice = chosen[...]
    spot = iota((128, 512), 0) == (cell[...] & 127)
    lines = [ready[0:1, :]]
    for f in range(3):
        lines.append(pick(split2(terms[f]), choice, spot))
    lines.append(ready[1:2, :])
    smooth = [{p: filter_xz(f, p) for p in range(1, 5)} for f in fields]
    numer = 0.0
    denom = 0.0
    for p in (2, 3):
        rate = strain(smooth, p)
        size = magnitude(rate)
        top, bottom = [], []
        for i, (a, b) in enumerate(PAIRS):
            product = {q: fields[a][q] * fields[b][q] for q in (p - 1, p, p + 1)}
            leonard = filter_xz(product, p) - smooth[a][p] * smooth[b][p]
            model = 2.0 * (filter_xz(tau[i], p) - 4.0 * size * rate[i])
            top.append(leonard * model)
            bottom.append(model * model)
        numer = numer + weighted(top)
        denom = denom + weighted(bottom)
    pad = jnp.zeros((32, 128), F32)
    both = jnp.concatenate([numer, denom, pad], axis=0).T
    total = jnp.sum(both, axis=0, keepdims=True)
    rows = [line[:, q * 128 : (q + 1) * 128] for line in lines for q in range(4)]
    block = jnp.concatenate(rows + [total, jnp.zeros((3, 128), F32)], axis=0)
    for i in range(message.shape[0] // LINES):
        message[i * LINES : (i + 1) * LINES, :] = block


def forecast_kernel(count, core, message, own, terms, send, state):
    parts = message.shape[0] // LINES
    total = jnp.sum(message[pl.ds(20, parts, stride=LINES), :], axis=0, keepdims=True)
    denom = pltpu.roll(total, 128 - 48, 1)
    coeff = (total / count) / (denom / count + 1e-6)
    coeff = jnp.where(iota((1, 128), 1) < 48, coeff, 0.0)
    column = jnp.broadcast_to(coeff, (128, 128)).T[:48]
    upper = shifted_y(column, 1)
    lower = shifted_y(column, -1)
    for a in range(3):
        for x in range(2):
            start = a * 96 + x * 48
            end = start + 48
            change = column * terms[0, start:end, :]
            change = change + (upper * terms[1, start:end, :] + lower * terms[2, start:end, :])
            state[start:end, :] = own[a, x] + change
    odd = core[0] == 1
    flow, height = [], []

    def lines(f):
        pieces = []
        for i in range(parts // 2):
            even_at = 2 * i * LINES + 4 * f
            odd_at = even_at + LINES
            pieces.append(jnp.where(odd, message[odd_at : odd_at + 4, :], message[even_at : even_at + 4, :]))
        return jnp.concatenate(pieces, axis=0)

    height = lines(4).astype(jnp.int32)
    table = jnp.broadcast_to(coeff, height.shape)

    def look(where):
        where = jnp.clip(where, 0, 127)
        return jnp.take_along_axis(table, where, axis=1)

    seen = lines(0) + look(height) * lines(1)
    seen = seen + (look(height + 1) * lines(2) + look(height - 1) * lines(3))
    for m in range(K):
        base = m * ROWS
        for a in range(3):
            send[base + 3 * a : base + 3 * a + 3, :] = state[a * 96 + 3 * m : a * 96 + 3 * m + 3, :]
        send[base + 9 : base + ROWS, :] = seen


def table_kernel(received, value, precision, table):
    member = iota((K, 128), 0)
    for i in range(8):
        parts = []
        for q in range(4):
            r = 4 * i + q
            seen = received[pl.ds(9 + r, K, stride=ROWS), :]
            mean = jnp.sum(seen, axis=0, keepdims=True) * (1.0 / K)
            innov = value[r : r + 1, :] - mean
            root = jnp.sqrt(precision[r : r + 1, :])
            parts.append(jnp.where(member == K - 1, innov, seen - mean) * root)
        table[i * 128 : (i + 1) * 128, :] = jnp.concatenate(parts, axis=0).T


def block_diagonal(value, mask):
    return jnp.concatenate([value] * 8, axis=0) * mask


def times_blocks(left, right, mask):
    r1, r2 = split2(right)
    l1, l2 = split2(left)
    rows = left.shape[0]
    wide = dot(jnp.concatenate([l1, l2], axis=0), block_diagonal(r1, mask))
    return wide[:rows] + wide[rows:] + dot(l1, block_diagonal(r2, mask))


def exact_times(left, constant):
    rows = left.shape[0]
    wide = dot(jnp.concatenate(split3(left), axis=0), constant)
    return (wide[2 * rows :] + wide[rows : 2 * rows]) + wide[:rows]


def weight_kernel(code, weights):
    columns = jnp.concatenate([code[...], jnp.zeros((96, 128), jnp.int32)], axis=0).T
    quarter = iota((LOC, 128), 1) // 32
    for c in range(CHUNKS):
        mark = jnp.broadcast_to(columns[:, c : c + 1], (LOC, 128))
        level = jnp.sqrt((mark & 15).astype(F32) * (1.0 / LEVELS))
        weights[c * LOC : (c + 1) * LOC, :] = jnp.where((mark >> 4) == quarter, level, 0.0)


def spread_kernel(received, tiles, centres, masks, chunks):
    tall = iota((256, 256), 0)
    wide_lane = iota((256, 256), 1)
    same = (tall // 32) == (wide_lane // 32)
    mask = jnp.where(same, 1.0, 0.0).astype(BF16)
    last = (wide_lane % 32) == 31
    not_last_row = (tall % 32) != 31
    rebuild = jnp.where(last, jnp.where(same & not_last_row, -1.0, 0.0), jnp.where(tall == wide_lane, 1.0, 0.0))
    masks[0] = mask
    masks[1] = rebuild.astype(BF16)
    cells = [received[pl.ds(r, K, stride=ROWS), :] for r in range(9)]
    means = [jnp.sum(v, axis=0, keepdims=True) * (1.0 / K) for v in cells]
    centres[...] = jnp.concatenate(means, axis=0)
    spreads = [v - m for v, m in zip(cells, means)]
    owner = iota((256, 288), 0) // 32
    chunk = (iota((256, 288), 1) % 32) // 4
    here = jnp.where(chunk == owner, 1.0, 0.0).astype(BF16)
    chunks[...] = here
    for g in range(4):
        packed = jnp.concatenate([v[:, 32 * g : 32 * g + 32] for v in spreads], axis=1)
        h1, h2 = split2(packed)
        tiles[g, :, 0:288] = block_diagonal(h1, here)
        tiles[g, :, 288:576] = block_diagonal(h2, here)


def folded(rows, weights):
    lone = rows * weights
    lone = lone + pltpu.roll(lone, 64, 1)
    return lone + pltpu.roll(lone, 32, 1)


def four_gram(pack):
    quarter = iota((LOC, 128), 1) // 32
    high, low = split2(pack)
    blocks = [jnp.where(quarter == i, 1.0, 0.0).astype(BF16) for i in range(4)]
    right1 = jnp.concatenate([high * b for b in blocks], axis=0)
    right2 = jnp.concatenate([low * b for b in blocks], axis=0)
    turned = pack.T
    turned = jnp.concatenate([turned[32 * i : 32 * i + 32] for i in range(4)], axis=1)
    left1, left2 = split2(turned)
    wide = dot(jnp.concatenate([left1, left2], axis=0), right1)
    return (wide[K:] + dot(left1, right2)) + wide[:K]


def analysis_kernel(places, weights, near, far, tiles, centres, masks, chunks, out, table, picked):
    table[0:1024, :] = near[...]
    table[1024:2048, :] = far[...]

    quarter = iota((LOC, 128), 1) // 32

    def fetch(at, carry):
        picked[pl.ds(at, 1), :] = table[pl.ds(places[at], 1), :]
        return carry

    lax.fori_loop(0, CHUNKS * LOC, fetch, 0, unroll=True)
    grams = []
    for four in range(CHUNKS // 4):
        pack = None
        for i in range(4):
            at = (4 * four + i) * LOC
            lone = folded(picked[at : at + LOC, :], weights[at : at + LOC, :])
            pack = lone if i == 0 else jnp.where(quarter == i, lone, pack)
        grams.append(four_gram(pack))
    packs = [jnp.concatenate([grams[2 * g], grams[2 * g + 1]], axis=1) for g in range(4)]

    mask = masks[0]
    rebuild = masks[1]
    member = iota((K, 256), 0)
    eye = jnp.where(member == iota((K, 256), 1) % 32, 1.0, 0.0)

    count = len(packs)
    drive, scale, y, z = [], [], [], []
    for g in range(count):
        pack = packs[g]
        body = jnp.where(member == K - 1, 0.0, pack)
        body = jnp.where(member == K - 1, -jnp.sum(body, axis=0, keepdims=True), body)
        push = jnp.broadcast_to(pack[K - 1 : K, :], (16, 256))
        whole = exact_times(jnp.concatenate([body, push], axis=0), rebuild)
        matrix = whole[:K] + ((K - 1) / 1.1) * eye
        square = jnp.broadcast_to(jnp.sum(matrix * matrix, axis=0, keepdims=True), (16, 256))
        norm = jnp.sqrt(exact_times(square, mask))
        rate = 1.0 / norm[0:1]
        push = whole[K:]
        both = times_blocks(jnp.concatenate([matrix, push], axis=0), matrix, mask)
        scaled = matrix * rate
        y.append(1.5 * scaled - (0.5 * rate * rate) * both[:K])
        z.append(1.5 * eye - 0.5 * scaled)
        drive.append(1.5 * push - (0.5 * rate) * both[K:])
        scale.append(jnp.sqrt(rate))
    for sweep in range(1, NS_ITERS):
        for g in range(count):
            factor = 1.5 * eye - 0.5 * times_blocks(z[g], y[g], mask)
            if sweep == NS_ITERS - 1:
                both = times_blocks(jnp.concatenate([z[g], drive[g]], axis=0), factor, mask)
                z[g], drive[g] = both[:K], both[K:]
            else:
                both = times_blocks(jnp.concatenate([y[g], z[g], drive[g]], axis=0), factor, mask)
                y[g], z[g], drive[g] = both[:K], both[K : 2 * K], both[2 * K :]
    moved = []
    for g in range(count):
        even = jnp.broadcast_to(scale[g] * (1.0 / K), (16, 256))
        spot = exact_times(jnp.concatenate([eye * drive[g][0:1], even], axis=0), chunks[...])
        pull, factor = spot[:K], spot[K : K + 1]
        left1, left2 = split2(z[g])
        part = dot(jnp.concatenate([left1, left2], axis=0), tiles[g])
        part = part[:K, :288] + part[K:, :288] + part[:K, 288:]
        mean = jnp.sum(pull * part, axis=0, keepdims=True) * (factor * factor)
        moved.append(part * (jnp.sqrt(float(K - 1)) * factor) + mean)
    for r in range(9):
        row = jnp.concatenate([part[:, 32 * r : 32 * r + 32] for part in moved], axis=1)
        out[pl.ds(r, K, stride=BACK), :] = row + centres[r : r + 1, :]


SCRATCH = [pltpu.VMEM((2048, 128), F32), pltpu.VMEM((CHUNKS * LOC, 128), F32)]


def order_kernel(returned, out):
    for m in range(K):
        x, y = m // 16, 3 * (m % 16)
        for a in range(3):
            out[a, x, y : y + 3, :] = returned[m * BACK + 3 * a : m * BACK + 3 * a + 3, :]


def call(kernel, shapes, ins, scratch=(), limit=24 * 2**20, kinds=None):
    return pl.pallas_call(
        kernel,
        out_shape=[jax.ShapeDtypeStruct(s, t) for s, t in zip(shapes, kinds or [F32] * len(shapes))],
        in_specs=ins,
        out_specs=[VMEM] * len(shapes),
        scratch_shapes=list(scratch),
        compiler_params=pltpu.CompilerParams(vmem_limit_bytes=limit),
    )


def exchange(rows, axis, count):
    width = rows.size // count
    sent = lax.all_to_all(rows.reshape(count, 1, width), axis, 0, 0, tiled=True)
    return sent.reshape(rows.shape)


def shards(ensemble, obs_cell, obs_comp, obs_value, obs_precision, loc_obs, loc_level):
    field = ensemble[0]
    _, depth, height, extent = field.shape
    parts = lax.axis_size("space")
    here = lax.axis_index("space")
    up = [(i, (i + 1) % parts) for i in range(parts)]
    down = [(j, i) for i, j in up]

    slab = loc_obs // 512
    within = loc_obs % 512
    places = (slab // 2) * 128 + ((slab + here) % 2) * 1024 + within % 128
    places = places.reshape(CHUNKS * LOC)
    code = (within // 128) * 16 + loc_level
    core = here & 1
    value = lax.dynamic_index_in_dim(obs_value.reshape(parts // 2, 2, 4, 128), core, 1, keepdims=False)
    value = value.reshape(K, 128)
    precision = lax.dynamic_index_in_dim(obs_precision.reshape(parts // 2, 2, 4, 128), core, 1, keepdims=False)
    precision = precision.reshape(K, 128)

    cell = obs_cell.reshape(1, 512)
    own, chosen, ready = call(
        first_kernel,
        [field.shape, (3 * depth * height, 512), (8, 512)],
        [pl.BlockSpec(memory_space=pl.ANY), VMEM, VMEM],
        kinds=[F32, BF16, F32],
    )(field, cell, obs_comp.reshape(1, 512))
    before = lax.ppermute(field, "space", up)
    after = lax.ppermute(field, "space", down)
    message, terms = call(
        model_kernel, [(parts * LINES, 128), (3, 3 * depth * height, extent)], [VMEM] * 6
    )(before, own, after, cell, chosen, ready)
    message = lax.all_to_all(message.reshape(parts, LINES, extent), "space", 0, 0, tiled=True)
    (weights,) = call(weight_kernel, [(CHUNKS * LOC, 128)], [VMEM])(code)
    message, weights, places = lax.optimization_barrier((message, weights, places))
    message = message.reshape(parts * LINES, extent)
    (send,) = call(
        functools.partial(forecast_kernel, depth * parts * extent),
        [(K * ROWS, 128)],
        [SMEM] + [VMEM] * 3,
        [pltpu.VMEM((3 * depth * height, extent), F32)],
    )(core.reshape(1), message, own, terms)
    received = exchange(send, "member", K)
    (near,) = call(table_kernel, [(parts * 64, 128)], [VMEM] * 3)(received, value, precision)
    far = lax.ppermute(near, "space", [(i, i ^ 1) for i in range(parts)])
    spread = call(
        spread_kernel,
        [(4, 256, 576), (9, 128), (2, 256, 256), (256, 288)],
        [VMEM],
        kinds=[BF16, F32, BF16, BF16],
    )(received)
    (result,) = call(
        analysis_kernel, [(K * BACK, 128)], [SMEM] + [VMEM] * 7, SCRATCH, 32 * 2**20
    )(places, weights, near, far, *spread)
    returned = exchange(result, "member", K)
    (result,) = call(order_kernel, [(3, depth, height, extent)], [VMEM])(returned)
    return result[None]


def solution(mesh):
    in_specs = (
        P("member", None, "space", None, None),
        P("space"),
        P("space"),
        P(),
        P(),
        P(("space", "member"), None),
        P(("space", "member"), None),
    )
    out_specs = P("member", None, "space", None, None)
    return jax.shard_map(shards, mesh=mesh, in_specs=in_specs, out_specs=out_specs, check_vma=False)
```

```python
import functools

import jax
import jax.numpy as jnp
from jax import lax
from jax.experimental import pallas as pl
from jax.experimental.pallas import tpu as pltpu
from jax.sharding import PartitionSpec as P

NS_ITERS = 8
LEVELS = 8
K = 32
LOC = 128
CHUNKS = 32
ROWS = 41
LINES = 24
BACK = 9

PAIRS = ((0, 0), (1, 1), (2, 2), (0, 1), (0, 2), (1, 2))
F32 = jnp.float32
BF16 = jnp.bfloat16
VMEM = pl.BlockSpec(memory_space=pltpu.VMEM)
SMEM = pl.BlockSpec(memory_space=pltpu.SMEM)


def iota(shape, dim):
    return lax.broadcasted_iota(jnp.int32, shape, dim)


def pair_index(first, second):
    return PAIRS.index((min(first, second), max(first, second)))


def split2(value):
    high = value.astype(BF16)
    return high, (value - high.astype(F32)).astype(BF16)


def split3(value):
    high = value.astype(BF16)
    rest = value - high.astype(F32)
    middle = rest.astype(BF16)
    return high, middle, (rest - middle.astype(F32)).astype(BF16)


def dot(left, right):
    return jnp.dot(left, right, preferred_element_type=F32)


def dot_t(left, right):
    return lax.dot_general(left, right, (((0,), (0,)), ((), ())), preferred_element_type=F32)


def along_y(plane):
    count = plane.shape[0]
    row = iota(plane.shape, 0)
    later = jnp.where(row == count - 1, 0.0, pltpu.roll(plane, count - 1, 0))
    earlier = jnp.where(row == 0, 0.0, pltpu.roll(plane, 1, 0))
    return 0.5 * (later - earlier)


def along_z(plane):
    count = plane.shape[1]
    return 0.5 * (pltpu.roll(plane, count - 1, 1) - pltpu.roll(plane, 1, 1))


def filter_z(plane):
    count = plane.shape[1]
    return 0.25 * (pltpu.roll(plane, 1, 1) + 2.0 * plane + pltpu.roll(plane, count - 1, 1))


def filter_xz(planes, p):
    return filter_z(0.25 * (planes[p - 1] + 2.0 * planes[p] + planes[p + 1]))


def strain(fields, p):
    grads = []
    for b in range(3):
        if b == 0:
            grads.append([0.5 * (f[p + 1] - f[p - 1]) for f in fields])
        elif b == 1:
            grads.append([along_y(f[p]) for f in fields])
        else:
            grads.append([along_z(f[p]) for f in fields])
    return [0.5 * (grads[b][a] + grads[a][b]) for a, b in PAIRS]


def weighted(terms):
    return terms[0] + terms[1] + terms[2] + 2.0 * (terms[3] + terms[4] + terms[5])


def magnitude(rate):
    return jnp.sqrt(2.0 * weighted([r * r for r in rate]))


def shifted_y(plane, step):
    count = plane.shape[0]
    row = iota(plane.shape, 0)
    if step > 0:
        return jnp.where(row == count - 1, 0.0, pltpu.roll(plane, count - 1, 0))
    return jnp.where(row == 0, 0.0, pltpu.roll(plane, 1, 0))


def pick(pieces, choice, spot):
    picked = dot_t(pieces[-1], choice)
    for piece in pieces[-2::-1]:
        picked = picked + dot_t(piece, choice)
    return jnp.sum(jnp.where(spot, picked, 0.0), axis=0, keepdims=True)


def first_kernel(source, cell, comp, own, chosen, ready):
    pltpu.sync_copy(source, own)
    level = cell[...] >> 7
    place = comp[...] * 96 + level
    choice = (iota((288, 512), 0) == place).astype(F32).astype(BF16)
    chosen[...] = choice
    spot = iota((128, 512), 0) == (cell[...] & 127)
    flow = pick(split3(own[...].reshape(288, 128)), choice, spot)
    level = jnp.where(level >= 48, level - 48, level).astype(F32)
    ready[...] = jnp.concatenate([flow, level, jnp.zeros((6, 512), F32)], axis=0)


def model_kernel(before, own, after, cell, chosen, ready, message, terms):
    fields = [
        {0: before[a, 0], 1: before[a, 1], 2: own[a, 0], 3: own[a, 1], 4: after[a, 0], 5: after[a, 1]}
        for a in range(3)
    ]
    tau = [{} for _ in PAIRS]
    for p in range(1, 5):
        rate = strain(fields, p)
        size = magnitude(rate)
        for i in range(6):
            tau[i][p] = size * rate[i]
    for a in range(3):
        for x in range(2):
            p = x + 2
            start = a * 96 + x * 48
            along = tau[pair_index(a, 0)]
            flat = 0.5 * (along[p + 1] - along[p - 1]) + along_z(tau[pair_index(a, 2)][p])
            upright = 0.25 * tau[pair_index(a, 1)][p]
            terms[0, start : start + 48, :] = 0.5 * flat
            terms[1, start : start + 48, :] = shifted_y(upright, 1)
            terms[2, start : start + 48, :] = -shifted_y(upright, -1)
    choice = chosen[...]
    spot = iota((128, 512), 0) == (cell[...] & 127)
    lines = [ready[0:1, :]]
    for f in range(3):
        lines.append(pick(split2(terms[f]), choice, spot))
    lines.append(ready[1:2, :])
    smooth = [{p: filter_xz(f, p) for p in range(1, 5)} for f in fields]
    numer = 0.0
    denom = 0.0
    for p in (2, 3):
        rate = strain(smooth, p)
        size = magnitude(rate)
        top, bottom = [], []
        for i, (a, b) in enumerate(PAIRS):
            product = {q: fields[a][q] * fields[b][q] for q in (p - 1, p, p + 1)}
            leonard = filter_xz(product, p) - smooth[a][p] * smooth[b][p]
            model = 2.0 * (filter_xz(tau[i], p) - 4.0 * size * rate[i])
            top.append(leonard * model)
            bottom.append(model * model)
        numer = numer + weighted(top)
        denom = denom + weighted(bottom)
    pad = jnp.zeros((32, 128), F32)
    both = jnp.concatenate([numer, denom, pad], axis=0).T
    total = jnp.sum(both, axis=0, keepdims=True)
    rows = [line[:, q * 128 : (q + 1) * 128] for line in lines for q in range(4)]
    block = jnp.concatenate(rows + [total, jnp.zeros((3, 128), F32)], axis=0)
    for i in range(message.shape[0] // LINES):
        message[i * LINES : (i + 1) * LINES, :] = block


def forecast_kernel(count, core, message, own, terms, send, state):
    parts = message.shape[0] // LINES
    total = jnp.sum(message[pl.ds(20, parts, stride=LINES), :], axis=0, keepdims=True)
    denom = pltpu.roll(total, 128 - 48, 1)
    coeff = (total / count) / (denom / count + 1e-6)
    coeff = jnp.where(iota((1, 128), 1) < 48, coeff, 0.0)
    column = jnp.broadcast_to(coeff, (128, 128)).T[:48]
    upper = shifted_y(column, 1)
    lower = shifted_y(column, -1)
    for a in range(3):
        for x in range(2):
            start = a * 96 + x * 48
            end = start + 48
            change = column * terms[0, start:end, :]
            change = change + (upper * terms[1, start:end, :] + lower * terms[2, start:end, :])
            state[start:end, :] = own[a, x] + change
    odd = core[0] == 1
    flow, height = [], []

    def lines(f):
        pieces = []
        for i in range(parts // 2):
            even_at = 2 * i * LINES + 4 * f
            odd_at = even_at + LINES
            pieces.append(jnp.where(odd, message[odd_at : odd_at + 4, :], message[even_at : even_at + 4, :]))
        return jnp.concatenate(pieces, axis=0)

    height = lines(4).astype(jnp.int32)
    table = jnp.broadcast_to(coeff, height.shape)

    def look(where):
        where = jnp.clip(where, 0, 127)
        return jnp.take_along_axis(table, where, axis=1)

    seen = lines(0) + look(height) * lines(1)
    seen = seen + (look(height + 1) * lines(2) + look(height - 1) * lines(3))
    for m in range(K):
        base = m * ROWS
        for a in range(3):
            send[base + 3 * a : base + 3 * a + 3, :] = state[a * 96 + 3 * m : a * 96 + 3 * m + 3, :]
        send[base + 9 : base + ROWS, :] = seen


def table_kernel(received, value, precision, table):
    member = iota((K, 128), 0)
    for i in range(8):
        parts = []
        for q in range(4):
            r = 4 * i + q
            seen = received[pl.ds(9 + r, K, stride=ROWS), :]
            mean = jnp.sum(seen, axis=0, keepdims=True) * (1.0 / K)
            innov = value[r : r + 1, :] - mean
            root = jnp.sqrt(precision[r : r + 1, :])
            parts.append(jnp.where(member == K - 1, innov, seen - mean) * root)
        table[i * 128 : (i + 1) * 128, :] = jnp.concatenate(parts, axis=0).T


def block_diagonal(value, mask):
    return jnp.concatenate([value] * 8, axis=0) * mask


def times_blocks(left, right, mask):
    r1, r2 = split2(right)
    l1, l2 = split2(left)
    rows = left.shape[0]
    wide = dot(jnp.concatenate([l1, l2], axis=0), block_diagonal(r1, mask))
    return wide[:rows] + wide[rows:] + dot(l1, block_diagonal(r2, mask))


def exact_times(left, constant):
    rows = left.shape[0]
    wide = dot(jnp.concatenate(split3(left), axis=0), constant)
    return (wide[2 * rows :] + wide[rows : 2 * rows]) + wide[:rows]


def weight_kernel(code, weights):
    columns = jnp.concatenate([code[...], jnp.zeros((96, 128), jnp.int32)], axis=0).T
    quarter = iota((LOC, 128), 1) // 32
    for c in range(CHUNKS):
        mark = jnp.broadcast_to(columns[:, c : c + 1], (LOC, 128))
        level = jnp.sqrt((mark & 15).astype(F32) * (1.0 / LEVELS))
        weights[c * LOC : (c + 1) * LOC, :] = jnp.where((mark >> 4) == quarter, level, 0.0)


def spread_kernel(received, tiles, centres, masks, chunks):
    tall = iota((256, 256), 0)
    wide_lane = iota((256, 256), 1)
    same = (tall // 32) == (wide_lane // 32)
    mask = jnp.where(same, 1.0, 0.0).astype(BF16)
    last = (wide_lane % 32) == 31
    not_last_row = (tall % 32) != 31
    rebuild = jnp.where(last, jnp.where(same & not_last_row, -1.0, 0.0), jnp.where(tall == wide_lane, 1.0, 0.0))
    masks[0] = mask
    masks[1] = rebuild.astype(BF16)
    cells = [received[pl.ds(r, K, stride=ROWS), :] for r in range(9)]
    means = [jnp.sum(v, axis=0, keepdims=True) * (1.0 / K) for v in cells]
    centres[...] = jnp.concatenate(means, axis=0)
    spreads = [v - m for v, m in zip(cells, means)]
    owner = iota((256, 288), 0) // 32
    chunk = (iota((256, 288), 1) % 32) // 4
    here = jnp.where(chunk == owner, 1.0, 0.0).astype(BF16)
    chunks[...] = here
    for g in range(4):
        packed = jnp.concatenate([v[:, 32 * g : 32 * g + 32] for v in spreads], axis=1)
        h1, h2 = split2(packed)
        tiles[g, :, 0:288] = block_diagonal(h1, here)
        tiles[g, :, 288:576] = block_diagonal(h2, here)


def folded(rows, weights):
    lone = rows * weights
    lone = lone + pltpu.roll(lone, 64, 1)
    return lone + pltpu.roll(lone, 32, 1)


def four_gram(pack):
    quarter = iota((LOC, 128), 1) // 32
    high, low = split2(pack)
    blocks = [jnp.where(quarter == i, 1.0, 0.0).astype(BF16) for i in range(4)]
    right1 = jnp.concatenate([high * b for b in blocks], axis=0)
    right2 = jnp.concatenate([low * b for b in blocks], axis=0)
    turned = pack.T
    turned = jnp.concatenate([turned[32 * i : 32 * i + 32] for i in range(4)], axis=1)
    left1, left2 = split2(turned)
    wide = dot(jnp.concatenate([left1, left2], axis=0), right1)
    return (wide[K:] + dot(left1, right2)) + wide[:K]


def analysis_kernel(places, weights, near, far, tiles, centres, masks, chunks, out, table, picked):
    table[0:1024, :] = near[...]
    table[1024:2048, :] = far[...]

    quarter = iota((LOC, 128), 1) // 32

    def fetch(at, carry):
        picked[pl.ds(at, 1), :] = table[pl.ds(places[at], 1), :]
        return carry

    lax.fori_loop(0, CHUNKS * LOC, fetch, 0, unroll=True)
    grams = []
    for four in range(CHUNKS // 4):
        pack = None
        for i in range(4):
            at = (4 * four + i) * LOC
            lone = folded(picked[at : at + LOC, :], weights[at : at + LOC, :])
            pack = lone if i == 0 else jnp.where(quarter == i, lone, pack)
        grams.append(four_gram(pack))
    packs = [jnp.concatenate([grams[2 * g], grams[2 * g + 1]], axis=1) for g in range(4)]

    mask = masks[0]
    rebuild = masks[1]
    member = iota((K, 256), 0)
    eye = jnp.where(member == iota((K, 256), 1) % 32, 1.0, 0.0)

    count = len(packs)
    drive, scale, y, z = [], [], [], []
    for g in range(count):
        pack = packs[g]
        body = jnp.where(member == K - 1, 0.0, pack)
        body = jnp.where(member == K - 1, -jnp.sum(body, axis=0, keepdims=True), body)
        push = jnp.broadcast_to(pack[K - 1 : K, :], (16, 256))
        whole = exact_times(jnp.concatenate([body, push], axis=0), rebuild)
        matrix = whole[:K] + ((K - 1) / 1.1) * eye
        square = jnp.broadcast_to(jnp.sum(matrix * matrix, axis=0, keepdims=True), (16, 256))
        norm = jnp.sqrt(exact_times(square, mask))
        rate = 1.0 / norm[0:1]
        push = whole[K:]
        both = times_blocks(jnp.concatenate([matrix, push], axis=0), matrix, mask)
        scaled = matrix * rate
        y.append(1.5 * scaled - (0.5 * rate * rate) * both[:K])
        z.append(1.5 * eye - 0.5 * scaled)
        drive.append(1.5 * push - (0.5 * rate) * both[K:])
        scale.append(jnp.sqrt(rate))
    for sweep in range(1, NS_ITERS):
        for g in range(count):
            factor = 1.5 * eye - 0.5 * times_blocks(z[g], y[g], mask)
            if sweep == NS_ITERS - 1:
                both = times_blocks(jnp.concatenate([z[g], drive[g]], axis=0), factor, mask)
                z[g], drive[g] = both[:K], both[K:]
            else:
                both = times_blocks(jnp.concatenate([y[g], z[g], drive[g]], axis=0), factor, mask)
                y[g], z[g], drive[g] = both[:K], both[K : 2 * K], both[2 * K :]
    moved = []
    for g in range(count):
        even = jnp.broadcast_to(scale[g] * (1.0 / K), (16, 256))
        spot = exact_times(jnp.concatenate([eye * drive[g][0:1], even], axis=0), chunks[...])
        pull, factor = spot[:K], spot[K : K + 1]
        left1, left2 = split2(z[g])
        part = dot(jnp.concatenate([left1, left2], axis=0), tiles[g])
        part = part[:K, :288] + part[K:, :288] + part[:K, 288:]
        mean = jnp.sum(pull * part, axis=0, keepdims=True) * (factor * factor)
        moved.append(part * (jnp.sqrt(float(K - 1)) * factor) + mean)
    for r in range(9):
        row = jnp.concatenate([part[:, 32 * r : 32 * r + 32] for part in moved], axis=1)
        out[pl.ds(r, K, stride=BACK), :] = row + centres[r : r + 1, :]


SCRATCH = [pltpu.VMEM((2048, 128), F32), pltpu.VMEM((CHUNKS * LOC, 128), F32)]


def order_kernel(returned, out):
    for m in range(K):
        x, y = m // 16, 3 * (m % 16)
        for a in range(3):
            out[a, x, y : y + 3, :] = returned[m * BACK + 3 * a : m * BACK + 3 * a + 3, :]


def call(kernel, shapes, ins, scratch=(), limit=24 * 2**20, kinds=None):
    return pl.pallas_call(
        kernel,
        out_shape=[jax.ShapeDtypeStruct(s, t) for s, t in zip(shapes, kinds or [F32] * len(shapes))],
        in_specs=ins,
        out_specs=[VMEM] * len(shapes),
        scratch_shapes=list(scratch),
        compiler_params=pltpu.CompilerParams(vmem_limit_bytes=limit),
    )


def exchange(rows, axis, count):
    width = rows.size // count
    sent = lax.all_to_all(rows.reshape(count, 1, width), axis, 0, 0, tiled=True)
    return sent.reshape(rows.shape)


def shards(ensemble, obs_cell, obs_comp, obs_value, obs_precision, loc_obs, loc_level):
    field = ensemble[0]
    _, depth, height, extent = field.shape
    parts = lax.axis_size("space")
    here = lax.axis_index("space")
    up = [(i, (i + 1) % parts) for i in range(parts)]
    down = [(j, i) for i, j in up]

    slab = loc_obs // 512
    within = loc_obs % 512
    places = (slab // 2) * 128 + ((slab + here) % 2) * 1024 + within % 128
    places = places.reshape(CHUNKS * LOC)
    code = (within // 128) * 16 + loc_level
    core = here & 1
    value = lax.dynamic_index_in_dim(obs_value.reshape(parts // 2, 2, 4, 128), core, 1, keepdims=False)
    value = value.reshape(K, 128)
    precision = lax.dynamic_index_in_dim(obs_precision.reshape(parts // 2, 2, 4, 128), core, 1, keepdims=False)
    precision = precision.reshape(K, 128)

    cell = obs_cell.reshape(1, 512)
    own, chosen, ready = call(
        first_kernel,
        [field.shape, (3 * depth * height, 512), (8, 512)],
        [pl.BlockSpec(memory_space=pl.ANY), VMEM, VMEM],
        kinds=[F32, BF16, F32],
    )(field, cell, obs_comp.reshape(1, 512))
    before = lax.ppermute(field, "space", up)
    after = lax.ppermute(field, "space", down)
    message, terms = call(
        model_kernel, [(parts * LINES, 128), (3, 3 * depth * height, extent)], [VMEM] * 6
    )(before, own, after, cell, chosen, ready)
    message = lax.all_to_all(message.reshape(parts, LINES, extent), "space", 0, 0, tiled=True)
    (weights,) = call(weight_kernel, [(CHUNKS * LOC, 128)], [VMEM])(code)
    message, weights, places, value, precision = lax.optimization_barrier(
        (message, weights, places, value, precision)
    )
    message = message.reshape(parts * LINES, extent)
    (send,) = call(
        functools.partial(forecast_kernel, depth * parts * extent),
        [(K * ROWS, 128)],
        [SMEM] + [VMEM] * 3,
        [pltpu.VMEM((3 * depth * height, extent), F32)],
    )(core.reshape(1), message, own, terms)
    received = exchange(send, "member", K)
    (near,) = call(table_kernel, [(parts * 64, 128)], [VMEM] * 3)(received, value, precision)
    far = lax.ppermute(near, "space", [(i, i ^ 1) for i in range(parts)])
    spread = call(
        spread_kernel,
        [(4, 256, 576), (9, 128), (2, 256, 256), (256, 288)],
        [VMEM],
        kinds=[BF16, F32, BF16, BF16],
    )(received)
    (result,) = call(
        analysis_kernel, [(K * BACK, 128)], [SMEM] + [VMEM] * 7, SCRATCH, 32 * 2**20
    )(places, weights, near, far, *spread)
    returned = exchange(result, "member", K)
    (result,) = call(order_kernel, [(3, depth, height, extent)], [VMEM])(returned)
    return result[None]


def solution(mesh):
    in_specs = (
        P("member", None, "space", None, None),
        P("space"),
        P("space"),
        P(),
        P(),
        P(("space", "member"), None),
        P(("space", "member"), None),
    )
    out_specs = P("member", None, "space", None, None)
    return jax.shard_map(shards, mesh=mesh, in_specs=in_specs, out_specs=out_specs, check_vma=False)
```

```python
import functools

import jax
import jax.numpy as jnp
from jax import lax
from jax.experimental import pallas as pl
from jax.experimental.pallas import tpu as pltpu
from jax.sharding import PartitionSpec as P

NS_ITERS = 8
LEVELS = 8
K = 32
LOC = 128
CHUNKS = 32
ROWS = 41
LINES = 24
BACK = 9

PAIRS = ((0, 0), (1, 1), (2, 2), (0, 1), (0, 2), (1, 2))
F32 = jnp.float32
BF16 = jnp.bfloat16
VMEM = pl.BlockSpec(memory_space=pltpu.VMEM)
SMEM = pl.BlockSpec(memory_space=pltpu.SMEM)


def iota(shape, dim):
    return lax.broadcasted_iota(jnp.int32, shape, dim)


def pair_index(first, second):
    return PAIRS.index((min(first, second), max(first, second)))


def split2(value):
    high = value.astype(BF16)
    return high, (value - high.astype(F32)).astype(BF16)


def split3(value):
    high = value.astype(BF16)
    rest = value - high.astype(F32)
    middle = rest.astype(BF16)
    return high, middle, (rest - middle.astype(F32)).astype(BF16)


def dot(left, right):
    return jnp.dot(left, right, preferred_element_type=F32)


def dot_t(left, right):
    return lax.dot_general(left, right, (((0,), (0,)), ((), ())), preferred_element_type=F32)


def along_y(plane):
    count = plane.shape[0]
    row = iota(plane.shape, 0)
    later = jnp.where(row == count - 1, 0.0, pltpu.roll(plane, count - 1, 0))
    earlier = jnp.where(row == 0, 0.0, pltpu.roll(plane, 1, 0))
    return 0.5 * (later - earlier)


def along_z(plane):
    count = plane.shape[1]
    return 0.5 * (pltpu.roll(plane, count - 1, 1) - pltpu.roll(plane, 1, 1))


def filter_z(plane):
    count = plane.shape[1]
    return 0.25 * (pltpu.roll(plane, 1, 1) + 2.0 * plane + pltpu.roll(plane, count - 1, 1))


def filter_xz(planes, p):
    return filter_z(0.25 * (planes[p - 1] + 2.0 * planes[p] + planes[p + 1]))


def strain(fields, p):
    grads = []
    for b in range(3):
        if b == 0:
            grads.append([0.5 * (f[p + 1] - f[p - 1]) for f in fields])
        elif b == 1:
            grads.append([along_y(f[p]) for f in fields])
        else:
            grads.append([along_z(f[p]) for f in fields])
    return [0.5 * (grads[b][a] + grads[a][b]) for a, b in PAIRS]


def weighted(terms):
    return terms[0] + terms[1] + terms[2] + 2.0 * (terms[3] + terms[4] + terms[5])


def magnitude(rate):
    return jnp.sqrt(2.0 * weighted([r * r for r in rate]))


def shifted_y(plane, step):
    count = plane.shape[0]
    row = iota(plane.shape, 0)
    if step > 0:
        return jnp.where(row == count - 1, 0.0, pltpu.roll(plane, count - 1, 0))
    return jnp.where(row == 0, 0.0, pltpu.roll(plane, 1, 0))


def pick(pieces, choice, spot):
    picked = dot_t(pieces[-1], choice)
    for piece in pieces[-2::-1]:
        picked = picked + dot_t(piece, choice)
    return jnp.sum(jnp.where(spot, picked, 0.0), axis=0, keepdims=True)


def first_kernel(source, cell, comp, own, chosen, ready):
    pltpu.sync_copy(source, own)
    level = cell[...] >> 7
    place = comp[...] * 96 + level
    choice = (iota((288, 512), 0) == place).astype(F32).astype(BF16)
    chosen[...] = choice
    spot = iota((128, 512), 0) == (cell[...] & 127)
    flow = pick(split3(own[...].reshape(288, 128)), choice, spot)
    level = jnp.where(level >= 48, level - 48, level).astype(F32)
    ready[...] = jnp.concatenate([flow, level, jnp.zeros((6, 512), F32)], axis=0)


def model_kernel(before, own, after, cell, chosen, ready, message, terms):
    fields = [
        {0: before[a, 0], 1: before[a, 1], 2: own[a, 0], 3: own[a, 1], 4: after[a, 0], 5: after[a, 1]}
        for a in range(3)
    ]
    tau = [{} for _ in PAIRS]
    for p in range(1, 5):
        rate = strain(fields, p)
        size = magnitude(rate)
        for i in range(6):
            tau[i][p] = size * rate[i]
    for a in range(3):
        for x in range(2):
            p = x + 2
            start = a * 96 + x * 48
            along = tau[pair_index(a, 0)]
            flat = 0.5 * (along[p + 1] - along[p - 1]) + along_z(tau[pair_index(a, 2)][p])
            upright = 0.25 * tau[pair_index(a, 1)][p]
            terms[0, start : start + 48, :] = 0.5 * flat
            terms[1, start : start + 48, :] = shifted_y(upright, 1)
            terms[2, start : start + 48, :] = -shifted_y(upright, -1)
    choice = chosen[...]
    spot = iota((128, 512), 0) == (cell[...] & 127)
    lines = [ready[0:1, :]]
    for f in range(3):
        lines.append(pick(split2(terms[f]), choice, spot))
    lines.append(ready[1:2, :])
    smooth = [{p: filter_xz(f, p) for p in range(1, 5)} for f in fields]
    numer = 0.0
    denom = 0.0
    for p in (2, 3):
        rate = strain(smooth, p)
        size = magnitude(rate)
        top, bottom = [], []
        for i, (a, b) in enumerate(PAIRS):
            product = {q: fields[a][q] * fields[b][q] for q in (p - 1, p, p + 1)}
            leonard = filter_xz(product, p) - smooth[a][p] * smooth[b][p]
            model = 2.0 * (filter_xz(tau[i], p) - 4.0 * size * rate[i])
            top.append(leonard * model)
            bottom.append(model * model)
        numer = numer + weighted(top)
        denom = denom + weighted(bottom)
    pad = jnp.zeros((32, 128), F32)
    both = jnp.concatenate([numer, denom, pad], axis=0).T
    total = jnp.sum(both, axis=0, keepdims=True)
    rows = [line[:, q * 128 : (q + 1) * 128] for line in lines for q in range(4)]
    block = jnp.concatenate(rows + [total, jnp.zeros((3, 128), F32)], axis=0)
    for i in range(message.shape[0] // LINES):
        message[i * LINES : (i + 1) * LINES, :] = block


def forecast_kernel(count, core, message, own, terms, send, state):
    parts = message.shape[0] // LINES
    total = jnp.sum(message[pl.ds(20, parts, stride=LINES), :], axis=0, keepdims=True)
    denom = pltpu.roll(total, 128 - 48, 1)
    coeff = (total / count) / (denom / count + 1e-6)
    coeff = jnp.where(iota((1, 128), 1) < 48, coeff, 0.0)
    column = jnp.broadcast_to(coeff, (128, 128)).T[:48]
    upper = shifted_y(column, 1)
    lower = shifted_y(column, -1)
    for a in range(3):
        for x in range(2):
            start = a * 96 + x * 48
            end = start + 48
            change = column * terms[0, start:end, :]
            change = change + (upper * terms[1, start:end, :] + lower * terms[2, start:end, :])
            state[start:end, :] = own[a, x] + change
    odd = core[0] == 1
    flow, height = [], []

    def lines(f):
        pieces = []
        for i in range(parts // 2):
            even_at = 2 * i * LINES + 4 * f
            odd_at = even_at + LINES
            pieces.append(jnp.where(odd, message[odd_at : odd_at + 4, :], message[even_at : even_at + 4, :]))
        return jnp.concatenate(pieces, axis=0)

    height = lines(4).astype(jnp.int32)
    table = jnp.broadcast_to(coeff, height.shape)

    def look(where):
        where = jnp.clip(where, 0, 127)
        return jnp.take_along_axis(table, where, axis=1)

    seen = lines(0) + look(height) * lines(1)
    seen = seen + (look(height + 1) * lines(2) + look(height - 1) * lines(3))
    for m in range(K):
        base = m * ROWS
        for a in range(3):
            send[base + 3 * a : base + 3 * a + 3, :] = state[a * 96 + 3 * m : a * 96 + 3 * m + 3, :]
        send[base + 9 : base + ROWS, :] = seen


def table_kernel(received, value, precision, table):
    member = iota((K, 128), 0)
    for i in range(8):
        parts = []
        for q in range(4):
            r = 4 * i + q
            seen = received[pl.ds(9 + r, K, stride=ROWS), :]
            mean = jnp.sum(seen, axis=0, keepdims=True) * (1.0 / K)
            innov = value[r : r + 1, :] - mean
            root = jnp.sqrt(precision[r : r + 1, :])
            parts.append(jnp.where(member == K - 1, innov, seen - mean) * root)
        table[i * 128 : (i + 1) * 128, :] = jnp.concatenate(parts, axis=0).T


def block_diagonal(value, mask):
    return jnp.concatenate([value] * 8, axis=0) * mask


def times_blocks(left, right, mask):
    r1, r2 = split2(right)
    l1, l2 = split2(left)
    rows = left.shape[0]
    wide = dot(jnp.concatenate([l1, l2], axis=0), block_diagonal(r1, mask))
    return wide[:rows] + wide[rows:] + dot(l1, block_diagonal(r2, mask))


def exact_times(left, constant):
    rows = left.shape[0]
    wide = dot(jnp.concatenate(split3(left), axis=0), constant)
    return (wide[2 * rows :] + wide[rows : 2 * rows]) + wide[:rows]


def weight_kernel(code, weights):
    columns = jnp.concatenate([code[...], jnp.zeros((96, 128), jnp.int32)], axis=0).T
    quarter = iota((LOC, 128), 1) // 32
    for c in range(CHUNKS):
        mark = jnp.broadcast_to(columns[:, c : c + 1], (LOC, 128))
        level = jnp.sqrt((mark & 15).astype(F32) * (1.0 / LEVELS))
        weights[c * LOC : (c + 1) * LOC, :] = jnp.where((mark >> 4) == quarter, level, 0.0)


def spread_kernel(received, tiles, centres, masks, chunks):
    tall = iota((256, 256), 0)
    wide_lane = iota((256, 256), 1)
    same = (tall // 32) == (wide_lane // 32)
    mask = jnp.where(same, 1.0, 0.0).astype(BF16)
    last = (wide_lane % 32) == 31
    not_last_row = (tall % 32) != 31
    rebuild = jnp.where(last, jnp.where(same & not_last_row, -1.0, 0.0), jnp.where(tall == wide_lane, 1.0, 0.0))
    masks[0] = mask
    masks[1] = rebuild.astype(BF16)
    cells = [received[pl.ds(r, K, stride=ROWS), :] for r in range(9)]
    means = [jnp.sum(v, axis=0, keepdims=True) * (1.0 / K) for v in cells]
    centres[...] = jnp.concatenate(means, axis=0)
    spreads = [v - m for v, m in zip(cells, means)]
    owner = iota((256, 288), 0) // 32
    chunk = (iota((256, 288), 1) % 32) // 4
    here = jnp.where(chunk == owner, 1.0, 0.0).astype(BF16)
    chunks[...] = here
    for g in range(4):
        packed = jnp.concatenate([v[:, 32 * g : 32 * g + 32] for v in spreads], axis=1)
        h1, h2 = split2(packed)
        tiles[g, :, 0:288] = block_diagonal(h1, here)
        tiles[g, :, 288:576] = block_diagonal(h2, here)


def folded(rows, weights):
    lone = rows * weights
    lone = lone + pltpu.roll(lone, 64, 1)
    return lone + pltpu.roll(lone, 32, 1)


def four_gram(pack):
    quarter = iota((LOC, 128), 1) // 32
    high, low = split2(pack)
    blocks = [jnp.where(quarter == i, 1.0, 0.0).astype(BF16) for i in range(4)]
    right1 = jnp.concatenate([high * b for b in blocks], axis=0)
    right2 = jnp.concatenate([low * b for b in blocks], axis=0)
    turned = pack.T
    turned = jnp.concatenate([turned[32 * i : 32 * i + 32] for i in range(4)], axis=1)
    left1, left2 = split2(turned)
    wide = dot(jnp.concatenate([left1, left2], axis=0), right1)
    return (wide[K:] + dot(left1, right2)) + wide[:K]


def analysis_kernel(places, weights, near, far, tiles, centres, masks, chunks, out, table, picked):
    table[0:1024, :] = near[...]
    table[1024:2048, :] = far[...]

    quarter = iota((LOC, 128), 1) // 32

    def fetch(at, carry):
        picked[pl.ds(at, 1), :] = table[pl.ds(places[at], 1), :]
        return carry

    lax.fori_loop(0, CHUNKS * LOC, fetch, 0, unroll=True)
    grams = []
    for four in range(CHUNKS // 4):
        pack = None
        for i in range(4):
            at = (4 * four + i) * LOC
            lone = folded(picked[at : at + LOC, :], weights[at : at + LOC, :])
            pack = lone if i == 0 else jnp.where(quarter == i, lone, pack)
        grams.append(four_gram(pack))
    packs = [jnp.concatenate([grams[2 * g], grams[2 * g + 1]], axis=1) for g in range(4)]

    mask = masks[0]
    rebuild = masks[1]
    member = iota((K, 256), 0)
    eye = jnp.where(member == iota((K, 256), 1) % 32, 1.0, 0.0)

    count = len(packs)
    drive, scale, y, z = [], [], [], []
    for g in range(count):
        pack = packs[g]
        body = jnp.where(member == K - 1, 0.0, pack)
        body = jnp.where(member == K - 1, -jnp.sum(body, axis=0, keepdims=True), body)
        push = jnp.broadcast_to(pack[K - 1 : K, :], (16, 256))
        whole = exact_times(jnp.concatenate([body, push], axis=0), rebuild)
        matrix = whole[:K] + ((K - 1) / 1.1) * eye
        square = jnp.broadcast_to(jnp.sum(matrix * matrix, axis=0, keepdims=True), (16, 256))
        norm = jnp.sqrt(exact_times(square, mask))
        rate = 1.0 / norm[0:1]
        push = whole[K:]
        both = times_blocks(jnp.concatenate([matrix, push], axis=0), matrix, mask)
        scaled = matrix * rate
        y.append(1.5 * scaled - (0.5 * rate * rate) * both[:K])
        z.append(1.5 * eye - 0.5 * scaled)
        drive.append(1.5 * push - (0.5 * rate) * both[K:])
        scale.append(jnp.sqrt(rate))
    for sweep in range(1, NS_ITERS):
        for g in range(count):
            factor = 1.5 * eye - 0.5 * times_blocks(z[g], y[g], mask)
            if sweep == NS_ITERS - 1:
                both = times_blocks(jnp.concatenate([z[g], drive[g]], axis=0), factor, mask)
                z[g], drive[g] = both[:K], both[K:]
            else:
                both = times_blocks(jnp.concatenate([y[g], z[g], drive[g]], axis=0), factor, mask)
                y[g], z[g], drive[g] = both[:K], both[K : 2 * K], both[2 * K :]
    moved = []
    for g in range(count):
        even = jnp.broadcast_to(scale[g] * (1.0 / K), (16, 256))
        spot = exact_times(jnp.concatenate([eye * drive[g][0:1], even], axis=0), chunks[...])
        pull, factor = spot[:K], spot[K : K + 1]
        left1, left2 = split2(z[g])
        part = dot(jnp.concatenate([left1, left2], axis=0), tiles[g])
        part = part[:K, :288] + part[K:, :288] + part[:K, 288:]
        mean = jnp.sum(pull * part, axis=0, keepdims=True) * (factor * factor)
        moved.append(part * (jnp.sqrt(float(K - 1)) * factor) + mean)
    for r in range(9):
        row = jnp.concatenate([part[:, 32 * r : 32 * r + 32] for part in moved], axis=1)
        out[pl.ds(r, K, stride=BACK), :] = row + centres[r : r + 1, :]


SCRATCH = [pltpu.VMEM((2048, 128), F32), pltpu.VMEM((CHUNKS * LOC, 128), F32)]


def order_kernel(returned, out):
    for m in range(K):
        x, y = m // 16, 3 * (m % 16)
        for a in range(3):
            out[a, x, y : y + 3, :] = returned[m * BACK + 3 * a : m * BACK + 3 * a + 3, :]


def call(kernel, shapes, ins, scratch=(), limit=24 * 2**20, kinds=None):
    return pl.pallas_call(
        kernel,
        out_shape=[jax.ShapeDtypeStruct(s, t) for s, t in zip(shapes, kinds or [F32] * len(shapes))],
        in_specs=ins,
        out_specs=[VMEM] * len(shapes),
        scratch_shapes=list(scratch),
        compiler_params=pltpu.CompilerParams(vmem_limit_bytes=limit),
    )


def exchange(rows, axis, count):
    width = rows.size // count
    sent = lax.all_to_all(rows.reshape(count, 1, width), axis, 0, 0, tiled=True)
    return sent.reshape(rows.shape)


def shards(ensemble, obs_cell, obs_comp, obs_value, obs_precision, loc_obs, loc_level):
    field = ensemble[0]
    _, depth, height, extent = field.shape
    parts = lax.axis_size("space")
    here = lax.axis_index("space")
    up = [(i, (i + 1) % parts) for i in range(parts)]
    down = [(j, i) for i, j in up]

    slab = loc_obs // 512
    within = loc_obs % 512
    places = (slab // 2) * 128 + ((slab + here) % 2) * 1024 + within % 128
    places = places.reshape(CHUNKS * LOC)
    code = (within // 128) * 16 + loc_level
    core = here & 1
    value = lax.dynamic_index_in_dim(obs_value.reshape(parts // 2, 2, 4, 128), core, 1, keepdims=False)
    value = value.reshape(K, 128)
    precision = lax.dynamic_index_in_dim(obs_precision.reshape(parts // 2, 2, 4, 128), core, 1, keepdims=False)
    precision = precision.reshape(K, 128)

    cell = obs_cell.reshape(1, 512)
    own, chosen, ready = call(
        first_kernel,
        [field.shape, (3 * depth * height, 512), (8, 512)],
        [pl.BlockSpec(memory_space=pl.ANY), VMEM, VMEM],
        kinds=[F32, BF16, F32],
    )(field, cell, obs_comp.reshape(1, 512))
    before = lax.ppermute(field, "space", up)
    after = lax.ppermute(field, "space", down)
    (weights,) = call(weight_kernel, [(CHUNKS * LOC, 128)], [VMEM])(code)
    own, weights, places, value, precision, core = lax.optimization_barrier(
        (own, weights, places, value, precision, core)
    )
    message, terms = call(
        model_kernel, [(parts * LINES, 128), (3, 3 * depth * height, extent)], [VMEM] * 6
    )(before, own, after, cell, chosen, ready)
    message = lax.all_to_all(message.reshape(parts, LINES, extent), "space", 0, 0, tiled=True)
    message = message.reshape(parts * LINES, extent)
    (send,) = call(
        functools.partial(forecast_kernel, depth * parts * extent),
        [(K * ROWS, 128)],
        [SMEM] + [VMEM] * 3,
        [pltpu.VMEM((3 * depth * height, extent), F32)],
    )(core.reshape(1), message, own, terms)
    received = exchange(send, "member", K)
    (near,) = call(table_kernel, [(parts * 64, 128)], [VMEM] * 3)(received, value, precision)
    far = lax.ppermute(near, "space", [(i, i ^ 1) for i in range(parts)])
    spread = call(
        spread_kernel,
        [(4, 256, 576), (9, 128), (2, 256, 256), (256, 288)],
        [VMEM],
        kinds=[BF16, F32, BF16, BF16],
    )(received)
    (result,) = call(
        analysis_kernel, [(K * BACK, 128)], [SMEM] + [VMEM] * 7, SCRATCH, 32 * 2**20
    )(places, weights, near, far, *spread)
    returned = exchange(result, "member", K)
    (result,) = call(order_kernel, [(3, depth, height, extent)], [VMEM])(returned)
    return result[None]


def solution(mesh):
    in_specs = (
        P("member", None, "space", None, None),
        P("space"),
        P("space"),
        P(),
        P(),
        P(("space", "member"), None),
        P(("space", "member"), None),
    )
    out_specs = P("member", None, "space", None, None)
    return jax.shard_map(shards, mesh=mesh, in_specs=in_specs, out_specs=out_specs, check_vma=False)
```

```python
import functools

import jax
import jax.numpy as jnp
from jax import lax
from jax.experimental import pallas as pl
from jax.experimental.pallas import tpu as pltpu
from jax.sharding import PartitionSpec as P

NS_ITERS = 8
LEVELS = 8
K = 32
LOC = 128
CHUNKS = 32
ROWS = 41
LINES = 24
BACK = 9

PAIRS = ((0, 0), (1, 1), (2, 2), (0, 1), (0, 2), (1, 2))
F32 = jnp.float32
BF16 = jnp.bfloat16
VMEM = pl.BlockSpec(memory_space=pltpu.VMEM)
SMEM = pl.BlockSpec(memory_space=pltpu.SMEM)


def iota(shape, dim):
    return lax.broadcasted_iota(jnp.int32, shape, dim)


def pair_index(first, second):
    return PAIRS.index((min(first, second), max(first, second)))


def split2(value):
    high = value.astype(BF16)
    return high, (value - high.astype(F32)).astype(BF16)


def split3(value):
    high = value.astype(BF16)
    rest = value - high.astype(F32)
    middle = rest.astype(BF16)
    return high, middle, (rest - middle.astype(F32)).astype(BF16)


def dot(left, right):
    return jnp.dot(left, right, preferred_element_type=F32)


def dot_t(left, right):
    return lax.dot_general(left, right, (((0,), (0,)), ((), ())), preferred_element_type=F32)


def along_y(plane):
    count = plane.shape[0]
    row = iota(plane.shape, 0)
    later = jnp.where(row == count - 1, 0.0, pltpu.roll(plane, count - 1, 0))
    earlier = jnp.where(row == 0, 0.0, pltpu.roll(plane, 1, 0))
    return 0.5 * (later - earlier)


def along_z(plane):
    count = plane.shape[1]
    return 0.5 * (pltpu.roll(plane, count - 1, 1) - pltpu.roll(plane, 1, 1))


def filter_z(plane):
    count = plane.shape[1]
    return 0.25 * (pltpu.roll(plane, 1, 1) + 2.0 * plane + pltpu.roll(plane, count - 1, 1))


def filter_xz(planes, p):
    return filter_z(0.25 * (planes[p - 1] + 2.0 * planes[p] + planes[p + 1]))


def strain(fields, p):
    grads = []
    for b in range(3):
        if b == 0:
            grads.append([0.5 * (f[p + 1] - f[p - 1]) for f in fields])
        elif b == 1:
            grads.append([along_y(f[p]) for f in fields])
        else:
            grads.append([along_z(f[p]) for f in fields])
    return [0.5 * (grads[b][a] + grads[a][b]) for a, b in PAIRS]


def weighted(terms):
    return terms[0] + terms[1] + terms[2] + 2.0 * (terms[3] + terms[4] + terms[5])


def magnitude(rate):
    return jnp.sqrt(2.0 * weighted([r * r for r in rate]))


def shifted_y(plane, step):
    count = plane.shape[0]
    row = iota(plane.shape, 0)
    if step > 0:
        return jnp.where(row == count - 1, 0.0, pltpu.roll(plane, count - 1, 0))
    return jnp.where(row == 0, 0.0, pltpu.roll(plane, 1, 0))


def pick(pieces, choice, spot):
    picked = dot_t(pieces[-1], choice)
    for piece in pieces[-2::-1]:
        picked = picked + dot_t(piece, choice)
    return jnp.sum(jnp.where(spot, picked, 0.0), axis=0, keepdims=True)


def first_kernel(source, cell, comp, own, chosen, ready):
    pltpu.sync_copy(source, own)
    level = cell[...] >> 7
    place = comp[...] * 96 + level
    choice = (iota((288, 512), 0) == place).astype(F32).astype(BF16)
    chosen[...] = choice
    spot = iota((128, 512), 0) == (cell[...] & 127)
    flow = pick(split3(own[...].reshape(288, 128)), choice, spot)
    level = jnp.where(level >= 48, level - 48, level).astype(F32)
    ready[...] = jnp.concatenate([flow, level, jnp.zeros((6, 512), F32)], axis=0)


def model_kernel(before, own, after, cell, chosen, ready, message, terms):
    fields = [
        {0: before[a, 0], 1: before[a, 1], 2: own[a, 0], 3: own[a, 1], 4: after[a, 0], 5: after[a, 1]}
        for a in range(3)
    ]
    tau = [{} for _ in PAIRS]
    for p in range(1, 5):
        rate = strain(fields, p)
        size = magnitude(rate)
        for i in range(6):
            tau[i][p] = size * rate[i]
    for a in range(3):
        for x in range(2):
            p = x + 2
            start = a * 96 + x * 48
            along = tau[pair_index(a, 0)]
            flat = 0.5 * (along[p + 1] - along[p - 1]) + along_z(tau[pair_index(a, 2)][p])
            upright = 0.25 * tau[pair_index(a, 1)][p]
            terms[0, start : start + 48, :] = 0.5 * flat
            terms[1, start : start + 48, :] = shifted_y(upright, 1)
            terms[2, start : start + 48, :] = -shifted_y(upright, -1)
    choice = chosen[...]
    spot = iota((128, 512), 0) == (cell[...] & 127)
    lines = [ready[0:1, :]]
    for f in range(3):
        lines.append(pick(split2(terms[f]), choice, spot))
    lines.append(ready[1:2, :])
    smooth = [{p: filter_xz(f, p) for p in range(1, 5)} for f in fields]
    numer = 0.0
    denom = 0.0
    for p in (2, 3):
        rate = strain(smooth, p)
        size = magnitude(rate)
        top, bottom = [], []
        for i, (a, b) in enumerate(PAIRS):
            product = {q: fields[a][q] * fields[b][q] for q in (p - 1, p, p + 1)}
            leonard = filter_xz(product, p) - smooth[a][p] * smooth[b][p]
            model = 2.0 * (filter_xz(tau[i], p) - 4.0 * size * rate[i])
            top.append(leonard * model)
            bottom.append(model * model)
        numer = numer + weighted(top)
        denom = denom + weighted(bottom)
    pad = jnp.zeros((32, 128), F32)
    both = jnp.concatenate([numer, denom, pad], axis=0).T
    total = jnp.sum(both, axis=0, keepdims=True)
    rows = [line[:, q * 128 : (q + 1) * 128] for line in lines for q in range(4)]
    block = jnp.concatenate(rows + [total, jnp.zeros((3, 128), F32)], axis=0)
    for i in range(message.shape[0] // LINES):
        message[i * LINES : (i + 1) * LINES, :] = block


def forecast_kernel(count, core, message, own, terms, send, state):
    parts = message.shape[0] // LINES
    total = jnp.sum(message[pl.ds(20, parts, stride=LINES), :], axis=0, keepdims=True)
    denom = pltpu.roll(total, 128 - 48, 1)
    coeff = (total / count) / (denom / count + 1e-6)
    coeff = jnp.where(iota((1, 128), 1) < 48, coeff, 0.0)
    column = jnp.broadcast_to(coeff, (128, 128)).T[:48]
    upper = shifted_y(column, 1)
    lower = shifted_y(column, -1)
    for a in range(3):
        for x in range(2):
            start = a * 96 + x * 48
            end = start + 48
            change = column * terms[0, start:end, :]
            change = change + (upper * terms[1, start:end, :] + lower * terms[2, start:end, :])
            state[start:end, :] = own[a, x] + change
    odd = core[0] == 1
    flow, height = [], []

    def lines(f):
        pieces = []
        for i in range(parts // 2):
            even_at = 2 * i * LINES + 4 * f
            odd_at = even_at + LINES
            pieces.append(jnp.where(odd, message[odd_at : odd_at + 4, :], message[even_at : even_at + 4, :]))
        return jnp.concatenate(pieces, axis=0)

    height = lines(4).astype(jnp.int32)
    table = jnp.broadcast_to(coeff, height.shape)

    def look(where):
        where = jnp.clip(where, 0, 127)
        return jnp.take_along_axis(table, where, axis=1)

    seen = lines(0) + look(height) * lines(1)
    seen = seen + (look(height + 1) * lines(2) + look(height - 1) * lines(3))
    for m in range(K):
        base = m * ROWS
        for a in range(3):
            send[base + 3 * a : base + 3 * a + 3, :] = state[a * 96 + 3 * m : a * 96 + 3 * m + 3, :]
        send[base + 9 : base + ROWS, :] = seen


def table_kernel(received, value, precision, table):
    member = iota((K, 128), 0)
    for i in range(8):
        parts = []
        for q in range(4):
            r = 4 * i + q
            seen = received[pl.ds(9 + r, K, stride=ROWS), :]
            mean = jnp.sum(seen, axis=0, keepdims=True) * (1.0 / K)
            innov = value[r : r + 1, :] - mean
            root = jnp.sqrt(precision[r : r + 1, :])
            parts.append(jnp.where(member == K - 1, innov, seen - mean) * root)
        table[i * 128 : (i + 1) * 128, :] = jnp.concatenate(parts, axis=0).T


def block_diagonal(value, mask):
    return jnp.concatenate([value] * 8, axis=0) * mask


def times_blocks(left, right, mask):
    r1, r2 = split2(right)
    l1, l2 = split2(left)
    rows = left.shape[0]
    wide = dot(jnp.concatenate([l1, l2], axis=0), block_diagonal(r1, mask))
    return wide[:rows] + wide[rows:] + dot(l1, block_diagonal(r2, mask))


def exact_times(left, constant):
    rows = left.shape[0]
    wide = dot(jnp.concatenate(split3(left), axis=0), constant)
    return (wide[2 * rows :] + wide[rows : 2 * rows]) + wide[:rows]


def weight_kernel(code, weights):
    columns = jnp.concatenate([code[...], jnp.zeros((96, 128), jnp.int32)], axis=0).T
    quarter = iota((LOC, 128), 1) // 32
    for c in range(CHUNKS):
        mark = jnp.broadcast_to(columns[:, c : c + 1], (LOC, 128))
        level = jnp.sqrt((mark & 15).astype(F32) * (1.0 / LEVELS))
        weights[c * LOC : (c + 1) * LOC, :] = jnp.where((mark >> 4) == quarter, level, 0.0)


def spread_kernel(received, tiles, centres, masks, chunks):
    tall = iota((256, 256), 0)
    wide_lane = iota((256, 256), 1)
    same = (tall // 32) == (wide_lane // 32)
    mask = jnp.where(same, 1.0, 0.0).astype(BF16)
    last = (wide_lane % 32) == 31
    not_last_row = (tall % 32) != 31
    rebuild = jnp.where(last, jnp.where(same & not_last_row, -1.0, 0.0), jnp.where(tall == wide_lane, 1.0, 0.0))
    masks[0] = mask
    masks[1] = rebuild.astype(BF16)
    cells = [received[pl.ds(r, K, stride=ROWS), :] for r in range(9)]
    means = [jnp.sum(v, axis=0, keepdims=True) * (1.0 / K) for v in cells]
    centres[...] = jnp.concatenate(means, axis=0)
    spreads = [v - m for v, m in zip(cells, means)]
    owner = iota((256, 288), 0) // 32
    chunk = (iota((256, 288), 1) % 32) // 4
    here = jnp.where(chunk == owner, 1.0, 0.0).astype(BF16)
    chunks[...] = here
    for g in range(4):
        packed = jnp.concatenate([v[:, 32 * g : 32 * g + 32] for v in spreads], axis=1)
        h1, h2 = split2(packed)
        tiles[g, :, 0:288] = block_diagonal(h1, here)
        tiles[g, :, 288:576] = block_diagonal(h2, here)


def folded(rows, weights):
    lone = rows * weights
    lone = lone + pltpu.roll(lone, 64, 1)
    return lone + pltpu.roll(lone, 32, 1)


def four_gram(pack):
    quarter = iota((LOC, 128), 1) // 32
    high, low = split2(pack)
    blocks = [jnp.where(quarter == i, 1.0, 0.0).astype(BF16) for i in range(4)]
    right1 = jnp.concatenate([high * b for b in blocks], axis=0)
    right2 = jnp.concatenate([low * b for b in blocks], axis=0)
    turned = pack.T
    turned = jnp.concatenate([turned[32 * i : 32 * i + 32] for i in range(4)], axis=1)
    left1, left2 = split2(turned)
    wide = dot(jnp.concatenate([left1, left2], axis=0), right1)
    return (wide[K:] + dot(left1, right2)) + wide[:K]


def analysis_kernel(places, weights, near, far, tiles, centres, masks, chunks, out, table, picked):
    table[0:1024, :] = near[...]
    table[1024:2048, :] = far[...]

    quarter = iota((LOC, 128), 1) // 32

    half = CHUNKS * LOC // 2

    def fetch(at, carry):
        both = places[at]
        picked[pl.ds(at, 1), :] = table[pl.ds(both & 65535, 1), :]
        picked[pl.ds(at + half, 1), :] = table[pl.ds(both >> 16, 1), :]
        return carry

    lax.fori_loop(0, half, fetch, 0, unroll=True)
    grams = []
    for four in range(CHUNKS // 4):
        pack = None
        for i in range(4):
            at = (4 * four + i) * LOC
            lone = folded(picked[at : at + LOC, :], weights[at : at + LOC, :])
            pack = lone if i == 0 else jnp.where(quarter == i, lone, pack)
        grams.append(four_gram(pack))
    packs = [jnp.concatenate([grams[2 * g], grams[2 * g + 1]], axis=1) for g in range(4)]

    mask = masks[0]
    rebuild = masks[1]
    member = iota((K, 256), 0)
    eye = jnp.where(member == iota((K, 256), 1) % 32, 1.0, 0.0)

    count = len(packs)
    drive, scale, y, z = [], [], [], []
    for g in range(count):
        pack = packs[g]
        body = jnp.where(member == K - 1, 0.0, pack)
        body = jnp.where(member == K - 1, -jnp.sum(body, axis=0, keepdims=True), body)
        push = jnp.broadcast_to(pack[K - 1 : K, :], (16, 256))
        whole = exact_times(jnp.concatenate([body, push], axis=0), rebuild)
        matrix = whole[:K] + ((K - 1) / 1.1) * eye
        square = jnp.broadcast_to(jnp.sum(matrix * matrix, axis=0, keepdims=True), (16, 256))
        norm = jnp.sqrt(exact_times(square, mask))
        rate = 1.0 / norm[0:1]
        push = whole[K:]
        both = times_blocks(jnp.concatenate([matrix, push], axis=0), matrix, mask)
        scaled = matrix * rate
        y.append(1.5 * scaled - (0.5 * rate * rate) * both[:K])
        z.append(1.5 * eye - 0.5 * scaled)
        drive.append(1.5 * push - (0.5 * rate) * both[K:])
        scale.append(jnp.sqrt(rate))
    for sweep in range(1, NS_ITERS):
        for g in range(count):
            factor = 1.5 * eye - 0.5 * times_blocks(z[g], y[g], mask)
            if sweep == NS_ITERS - 1:
                both = times_blocks(jnp.concatenate([z[g], drive[g]], axis=0), factor, mask)
                z[g], drive[g] = both[:K], both[K:]
            else:
                both = times_blocks(jnp.concatenate([y[g], z[g], drive[g]], axis=0), factor, mask)
                y[g], z[g], drive[g] = both[:K], both[K : 2 * K], both[2 * K :]
    moved = []
    for g in range(count):
        even = jnp.broadcast_to(scale[g] * (1.0 / K), (16, 256))
        spot = exact_times(jnp.concatenate([eye * drive[g][0:1], even], axis=0), chunks[...])
        pull, factor = spot[:K], spot[K : K + 1]
        left1, left2 = split2(z[g])
        part = dot(jnp.concatenate([left1, left2], axis=0), tiles[g])
        part = part[:K, :288] + part[K:, :288] + part[:K, 288:]
        mean = jnp.sum(pull * part, axis=0, keepdims=True) * (factor * factor)
        moved.append(part * (jnp.sqrt(float(K - 1)) * factor) + mean)
    for r in range(9):
        row = jnp.concatenate([part[:, 32 * r : 32 * r + 32] for part in moved], axis=1)
        out[pl.ds(r, K, stride=BACK), :] = row + centres[r : r + 1, :]


SCRATCH = [pltpu.VMEM((2048, 128), F32), pltpu.VMEM((CHUNKS * LOC, 128), F32)]


def order_kernel(returned, out):
    for m in range(K):
        x, y = m // 16, 3 * (m % 16)
        for a in range(3):
            out[a, x, y : y + 3, :] = returned[m * BACK + 3 * a : m * BACK + 3 * a + 3, :]


def call(kernel, shapes, ins, scratch=(), limit=24 * 2**20, kinds=None):
    return pl.pallas_call(
        kernel,
        out_shape=[jax.ShapeDtypeStruct(s, t) for s, t in zip(shapes, kinds or [F32] * len(shapes))],
        in_specs=ins,
        out_specs=[VMEM] * len(shapes),
        scratch_shapes=list(scratch),
        compiler_params=pltpu.CompilerParams(vmem_limit_bytes=limit),
    )


def exchange(rows, axis, count):
    width = rows.size // count
    sent = lax.all_to_all(rows.reshape(count, 1, width), axis, 0, 0, tiled=True)
    return sent.reshape(rows.shape)


def shards(ensemble, obs_cell, obs_comp, obs_value, obs_precision, loc_obs, loc_level):
    field = ensemble[0]
    _, depth, height, extent = field.shape
    parts = lax.axis_size("space")
    here = lax.axis_index("space")
    up = [(i, (i + 1) % parts) for i in range(parts)]
    down = [(j, i) for i, j in up]

    slab = loc_obs // 512
    within = loc_obs % 512
    places = (slab // 2) * 128 + ((slab + here) % 2) * 1024 + within % 128
    places = (places[: CHUNKS // 2] + places[CHUNKS // 2 :] * 65536).reshape(CHUNKS * LOC // 2)
    code = (within // 128) * 16 + loc_level
    core = here & 1
    value = lax.dynamic_index_in_dim(obs_value.reshape(parts // 2, 2, 4, 128), core, 1, keepdims=False)
    value = value.reshape(K, 128)
    precision = lax.dynamic_index_in_dim(obs_precision.reshape(parts // 2, 2, 4, 128), core, 1, keepdims=False)
    precision = precision.reshape(K, 128)

    cell = obs_cell.reshape(1, 512)
    own, chosen, ready = call(
        first_kernel,
        [field.shape, (3 * depth * height, 512), (8, 512)],
        [pl.BlockSpec(memory_space=pl.ANY), VMEM, VMEM],
        kinds=[F32, BF16, F32],
    )(field, cell, obs_comp.reshape(1, 512))
    before = lax.ppermute(field, "space", up)
    after = lax.ppermute(field, "space", down)
    (weights,) = call(weight_kernel, [(CHUNKS * LOC, 128)], [VMEM])(code)
    own, weights, places, value, precision, core = lax.optimization_barrier(
        (own, weights, places, value, precision, core)
    )
    message, terms = call(
        model_kernel, [(parts * LINES, 128), (3, 3 * depth * height, extent)], [VMEM] * 6
    )(before, own, after, cell, chosen, ready)
    message = lax.all_to_all(message.reshape(parts, LINES, extent), "space", 0, 0, tiled=True)
    message = message.reshape(parts * LINES, extent)
    (send,) = call(
        functools.partial(forecast_kernel, depth * parts * extent),
        [(K * ROWS, 128)],
        [SMEM] + [VMEM] * 3,
        [pltpu.VMEM((3 * depth * height, extent), F32)],
    )(core.reshape(1), message, own, terms)
    received = exchange(send, "member", K)
    (near,) = call(table_kernel, [(parts * 64, 128)], [VMEM] * 3)(received, value, precision)
    far = lax.ppermute(near, "space", [(i, i ^ 1) for i in range(parts)])
    spread = call(
        spread_kernel,
        [(4, 256, 576), (9, 128), (2, 256, 256), (256, 288)],
        [VMEM],
        kinds=[BF16, F32, BF16, BF16],
    )(received)
    (result,) = call(
        analysis_kernel, [(K * BACK, 128)], [SMEM] + [VMEM] * 7, SCRATCH, 32 * 2**20
    )(places, weights, near, far, *spread)
    returned = exchange(result, "member", K)
    (result,) = call(order_kernel, [(3, depth, height, extent)], [VMEM])(returned)
    return result[None]


def solution(mesh):
    in_specs = (
        P("member", None, "space", None, None),
        P("space"),
        P("space"),
        P(),
        P(),
        P(("space", "member"), None),
        P(("space", "member"), None),
    )
    out_specs = P("member", None, "space", None, None)
    return jax.shard_map(shards, mesh=mesh, in_specs=in_specs, out_specs=out_specs, check_vma=False)
```
